32 devices in a mesh: groups: 2 (over y), lon: 4 (over z), lat: 2 (over x), cl: 2 (over core).
Axes of the slice: x: 2, y: 2, z: 4, core: 2. Of those that a mesh axis runs over, the one named last changes fastest.
Arguments:
- ocean_state: float32 [8, 32, 8, 1024], P('groups', None, 'lat', ('lon', 'cl')), parts along dimension 0, may hold values from -6 to 6
- cotangent: float32 [8, 32, 8, 1024], P('groups', None, 'lat', ('lon', 'cl')), parts along dimension 0, may hold values from -6 to 6
- diffusivity: float32 [32, 8, 1024], P(None, 'lat', ('lon', 'cl')), may hold values from 0.02 to 0.24
- east_peclet: float32 [32, 8, 1024], P(None, 'lat', ('lon', 'cl')), may hold values from -0.9 to 0.9
- north_peclet: float32 [32, 8, 1024], P(None, 'lat', ('lon', 'cl')), may hold values from -0.9 to 0.9
- sea_mask: int32 [8, 1024], P('lat', ('lon', 'cl')), may hold values 0 or 1
- depth_levels: int32 [8, 1024], P('lat', ('lon', 'cl')), may hold values from 1 to 32
- owner_table: int32 [2, 8, 512, 1], P('lat', ('lon', 'cl')), may hold values from 0 to 7; in each aligned block of 512 rows (0 to 511, 512 to 1023, ..., all dimensions but the last counted through in order) at most 128 rows name the same one
- w_in: bfloat16 [8, 128, 256], P(('lon', 'lat')), may hold values from -0.5 to 0.5
- w_mid: bfloat16 [8, 1, 256, 256], P(('lon', 'lat')), may hold values from -0.375 to 0.375
- w_out: bfloat16 [8, 256, 128], P(('lon', 'lat')), may hold values from -0.375 to 0.375
Outputs:
- advected: float32 [8, 32, 8, 1024], P('groups', None, 'lat', ('lon', 'cl')), parts along dimension 0
- tendency: bfloat16 [8, 32, 8, 1024], P('groups', None, 'lat', ('lon', 'cl')), parts along dimension 0
- state_grad: float32 [8, 32, 8, 1024], P('groups', None, 'lat', ('lon', 'cl')), parts along dimension 0
- grad_w_in: float32 [16, 128, 256], P(('groups', 'lon', 'lat')), parts along dimension 0
- grad_w_mid: float32 [16, 1, 256, 256], P(('groups', 'lon', 'lat')), parts along dimension 0
- grad_w_out: float32 [16, 256, 128], P(('groups', 'lon', 'lat')), parts along dimension 0
The draws below stay inside these ranges and needn't reach their ends.
There are 2 independent parts, one for each index of `groups`. The reference program is written for one: setup_inputs(seed, part) draws one part's arguments, and reference() takes and returns one part's arrays. A program takes and returns all parts, laid end to end along the dimension named above; an argument that names none is the same for every part. Nothing has to cross between parts.
Inputs may be any that keep to these rules, and one draw needn't show every extreme that they name: `owner_table`: in each device's block of 512 columns of the table, no region is named more than 128 times.
All inputs are finite; a program needn't handle non-finite values. No bound on the sum of `sea_mask` on one device may be relied on, other than what follows from the above.
Results may differ from the reference program's by a relative error of at most 0.0068.
Values may be sent and summed in bfloat16 or wider, within the bound.
A program may use at most 64 MiB of HBM per device.

```python
import math
import jax
import jax.numpy as jnp
import numpy as np
from jax import lax

LEVELS = 32
HIDDEN_SIZE = 256
DEPTH = 1
STEPS = 2
CLAT = 4
CLON = 128
FEATS = 128
EXPERTS = 8
CAP = 128
NLAT = 8
NLON = 1024
N_LON = 4
N_LAT = 2
N_CL = 2


def place_ends(entries, key, smallest, high):
    extent = entries.shape
    place = [jax.random.randint(jax.random.fold_in(key, axis), (), 0, extent[axis]) for axis in range(len(extent))]
    entries = entries.at[tuple(place)].set(smallest)
    longest = extent.index(max(extent))
    place[longest] = (place[longest] + 1) % extent[longest]
    return entries.at[tuple(place)].set(high)


def shard_levels(rng, dims, shards, least, high):
    def one(position, shards_of):
        steps = jax.random.uniform(jax.random.fold_in(jax.random.fold_in(rng, 6), position), (shards_of,), jnp.float32, least / len(shards), high / len(shards))
        return jnp.repeat(jnp.exp(steps), dims[position] // shards_of).reshape((-1,) + (1,) * (len(dims) - position - 1))

    gain = one(*shards[0])
    for cut in shards[1:]:
        gain = gain * one(*cut)
    return gain


def deal_out(own_key, own, number, rows, count, top, limit, lean):
    ranking = jax.random.permutation(own_key, count)
    packed, ordinary = load_shares(count, rows * top, limit, lean, True), load_shares(count, rows * top, limit, lean, False)
    places = jnp.arange(count)

    def named(tallies, turn):
        used = int((tallies > 0).sum())
        fixed = max(1, used // 4)
        moved = fixed + (places - fixed + turn * (used - fixed)) % max(1, count - fixed)
        return jnp.zeros((count,), jnp.int32).at[ranking[jnp.where(places < fixed, places, moved)]].set(jnp.asarray(tallies, jnp.int32))

    tallies = jnp.where(number % 4 == 0, named(packed, number // 4), named(ordinary, number - number // 4 - 1))
    mixed = jax.random.permutation(jax.random.fold_in(own, 3), count)
    giver, taker = mixed[0:count // 2 * 2:2], mixed[1:count // 2 * 2:2]
    room = jnp.minimum(tallies[giver] - 1, limit - tallies[taker]) // 2
    room = jnp.where((giver == ranking[0]) | (taker == ranking[0]) | (tallies[taker] == 0), 0, jnp.maximum(room, 0))
    moved = jax.random.randint(jax.random.fold_in(own, 4), (count // 2,), 0, 1 << 20) % (room + 1)
    tallies = tallies.at[giver].add(-moved).at[taker].add(moved)
    members = jnp.searchsorted(jnp.cumsum(tallies), jnp.arange(rows * top), side="right").astype(jnp.int32)
    listing = members.reshape(top, rows).T
    listing = listing[jax.random.permutation(jax.random.fold_in(own, 1), rows)]
    turn = jax.random.randint(jax.random.fold_in(own, 2), (rows, 1), 0, top)
    return jnp.take_along_axis(listing, (jnp.arange(top)[None, :] + turn) % top, axis=1)


def load_shares(number_of, total, limit, skew, full):
    loads = [(1 << 20) // math.isqrt(standing ** skew) + 1 for standing in range(1, number_of + 1)]
    largest = limit if full else min(limit, max(-(-total // number_of), total * loads[0] // sum(loads)))
    least = 1 if total - largest >= number_of - 1 else 0
    counts, surplus = [largest] + [least] * (number_of - 1), total - largest - least * (number_of - 1)
    while surplus > 0:
        movable = [i for i in range(1, number_of) if counts[i] < largest] or [i for i in range(1, number_of) if counts[i] < limit]
        whole, remaining = sum([loads[i] for i in movable]), surplus
        for i in movable:
            addition = min(limit - counts[i], max(1, remaining * loads[i] // whole), surplus)
            counts[i] = counts[i] + addition
            surplus = surplus - addition
    return np.array(counts)


def gaussian(own_key, dims, width, reach, pieces=(), kind=jnp.bfloat16):
    level = shard_levels(own_key, dims, pieces, -0.22, 0.18) if pieces else 1.0
    result = jax.random.normal(own_key, dims, jnp.float32) * width * level
    return jnp.minimum(jnp.maximum(result, -reach), reach).astype(kind)


def setup_inputs(seed: int = 0, part: int = 0) -> dict:
    splits = jax.random.split(jax.random.key(seed), 12)
    part_keys = jax.random.split(jax.random.fold_in(splits[11], part), 12)
    ocean_state = gaussian(part_keys[0], (4, LEVELS, NLAT, NLON), 1.0, 6.0, ((2, 2), (3, 8)), jnp.float32)
    cotangent = gaussian(part_keys[1], (4, LEVELS, NLAT, NLON), 1.0, 6.0, ((2, 2), (3, 8)), jnp.float32)
    diffusivity = jnp.clip(jnp.exp(math.log(0.24) - 2.4849066 * jax.random.uniform(splits[2], (LEVELS, NLAT, NLON), jnp.float32) ** shard_levels(splits[2], (LEVELS, NLAT, NLON), ((1, 2), (2, 8)), -0.2, 0.2)), 0.02, 0.24)
    east_peclet = jnp.clip(jax.random.uniform(splits[3], (LEVELS, NLAT, NLON), jnp.float32, -0.9, 0.9) * shard_levels(splits[3], (LEVELS, NLAT, NLON), ((1, 2), (2, 8)), -0.4, 0.0), -0.9, 0.9)
    north_peclet = jnp.clip(jax.random.uniform(splits[4], (LEVELS, NLAT, NLON), jnp.float32, -0.9, 0.9) * shard_levels(splits[4], (LEVELS, NLAT, NLON), ((1, 2), (2, 8)), -0.4, 0.0), -0.9, 0.9)
    sea_mask = place_ends((jax.random.randint(splits[5], (NLAT, NLON), 0, 4) < 3).astype(jnp.int32), jax.random.fold_in(splits[5], 1), 0, 1)
    depth_levels = place_ends(jax.random.randint(splits[6], (NLAT, NLON), 1, LEVELS + 1), jax.random.fold_in(splits[6], 1), 1, LEVELS).astype(jnp.int32)
    owner_table_keys = jax.random.split(jax.random.fold_in(splits[7], 1), N_LAT * (N_LON * N_CL) * (CLAT * CLON) // (CLAT * CLON))
    owner_table_turns = jax.random.permutation(jax.random.fold_in(splits[7], 3), N_LAT * (N_LON * N_CL) * (CLAT * CLON) // (CLAT * CLON))
    owner_table = jax.vmap(lambda own, number: deal_out(jax.random.fold_in(splits[7], 2), own, number, CLAT * CLON, EXPERTS, 1, CAP, 2))(owner_table_keys, owner_table_turns).reshape((N_LAT, N_LON * N_CL, CLAT * CLON, 1))
    w_in = gaussian(splits[8], (EXPERTS, FEATS, HIDDEN_SIZE), FEATS ** -0.5, 0.5, ((0, 8),))
    w_mid = gaussian(splits[9], (EXPERTS, DEPTH, HIDDEN_SIZE, HIDDEN_SIZE), HIDDEN_SIZE ** -0.5, 0.375, ((0, 8),))
    w_out = gaussian(splits[10], (EXPERTS, HIDDEN_SIZE, FEATS), HIDDEN_SIZE ** -0.5, 0.375, ((0, 8),))
    return {"ocean_state": ocean_state, "cotangent": cotangent, "diffusivity": diffusivity, "east_peclet": east_peclet, "north_peclet": north_peclet, "sea_mask": sea_mask, "depth_levels": depth_levels, "owner_table": owner_table, "w_in": w_in, "w_mid": w_mid, "w_out": w_out}


def build_table(diffusivity, east_peclet, north_peclet, sea_mask, depth_levels):
    levels = lax.broadcasted_iota(jnp.int32, diffusivity.shape, 0)
    active = (levels < depth_levels[None]).astype(jnp.float32) * sea_mask[None].astype(jnp.float32)
    return jnp.stack([diffusivity * (1.0 - east_peclet), diffusivity * (1.0 + east_peclet),
                      diffusivity * (1.0 - north_peclet), diffusivity * (1.0 + north_peclet),
                      4.0 * diffusivity, active])


def shifted(grid_values, lat_by, lon_by):
    if lon_by != 0:
        grid_values = jnp.roll(grid_values, -lon_by, axis=-1)
    zero_row = jnp.zeros_like(grid_values[..., :1, :])
    if lat_by == 1:
        grid_values = jnp.concatenate([grid_values[..., 1:, :], zero_row], axis=-2)
    if lat_by == -1:
        grid_values = jnp.concatenate([zero_row, grid_values[..., :-1, :]], axis=-2)
    return grid_values


def advance_whole(grid_values, coefficients):
    change = coefficients[0] * shifted(grid_values, 0, 1) + coefficients[1] * shifted(grid_values, 0, -1)
    change = change + coefficients[2] * shifted(grid_values, 1, 0) + coefficients[3] * shifted(grid_values, -1, 0)
    return grid_values + coefficients[5] * (change - coefficients[4] * grid_values)


def retreat_whole(grid_values, coefficients):
    pushed = coefficients[5] * grid_values
    summed = grid_values - coefficients[4] * pushed
    summed = summed + shifted(coefficients[0] * pushed, 0, -1) + shifted(coefficients[1] * pushed, 0, 1)
    summed = summed + shifted(coefficients[2] * pushed, -1, 0) + shifted(coefficients[3] * pushed, 1, 0)
    return summed


def project(left, right):
    return jnp.dot(left.astype(jnp.float32), right.astype(jnp.float32), preferred_element_type=jnp.float32)


def closure_pass(inputs, pushed, w_in, w_mid, w_out):
    slopes = []
    layers = [inputs]
    shaped = jnp.tanh(project(inputs, w_in))
    slopes.append(1.0 - shaped * shaped)
    acting = shaped.astype(jnp.bfloat16)
    layers.append(acting)
    for layer_index in range(w_mid.shape[0]):
        shaped = jnp.tanh(project(acting, w_mid[layer_index]))
        slopes.append(1.0 - shaped * shaped)
        acting = shaped.astype(jnp.bfloat16)
        layers.append(acting)
    raw_tend = project(acting, w_out).astype(jnp.bfloat16)
    grad_out = project(acting.T, pushed)
    backward = project(pushed, w_out.T)
    mid_grads = []
    for layer_index in reversed(range(w_mid.shape[0])):
        deltas = (backward * slopes[layer_index + 1]).astype(jnp.bfloat16)
        mid_grads.append(project(layers[layer_index + 1].T, deltas))
        backward = project(deltas, w_mid[layer_index].T)
    deltas = (backward * slopes[0]).astype(jnp.bfloat16)
    grad_in = project(inputs.T, deltas)
    back_in = project(deltas, w_in.T).astype(jnp.bfloat16)
    return raw_tend, back_in, grad_in, jnp.stack(mid_grads[::-1]), grad_out


def reference(ocean_state, cotangent, diffusivity, east_peclet, north_peclet, sea_mask, depth_levels, owner_table, w_in, w_mid, w_out):
    coefficients = build_table(diffusivity, east_peclet, north_peclet, sea_mask, depth_levels)
    active = coefficients[5]
    advected = ocean_state
    for number in range(STEPS):
        advected = advance_whole(advected, coefficients)
    sources = N_LAT * N_LON * N_CL
    experts = N_LON * N_LAT
    columns = CLAT * CLON
    lon_blocks = N_LON * N_CL

    def to_blocks(whole):
        shaped = whole.reshape(FEATS, N_LAT, CLAT, lon_blocks, CLON)
        return shaped.transpose(1, 3, 2, 4, 0).reshape(sources * columns, FEATS)

    def from_blocks(rows):
        shaped = rows.reshape(N_LAT, lon_blocks, CLAT, CLON, FEATS)
        return shaped.transpose(4, 0, 2, 1, 3).reshape(4, LEVELS, NLAT, NLON)

    owners = owner_table.reshape(sources, columns).astype(jnp.int32)
    one_hot = (owners[:, :, None] == jnp.arange(experts, dtype=jnp.int32)[None, None, :]).astype(jnp.int32)
    rank_in = jnp.sum(jnp.cumsum(one_hot, axis=1) * one_hot, axis=2) - 1
    source_ids = jnp.arange(sources, dtype=jnp.int32)[:, None]
    slot_index = ((owners * sources + source_ids) * CAP + rank_in).reshape(-1).astype(jnp.int32)
    col_inputs = to_blocks(advected).astype(jnp.bfloat16)
    col_pushed = to_blocks(active[None] * cotangent).astype(jnp.bfloat16)
    empty = jnp.zeros((experts * sources * CAP, FEATS), jnp.bfloat16)
    buffer_in = empty.at[slot_index].set(col_inputs).reshape(experts, sources * CAP, FEATS)
    buffer_pushed = empty.at[slot_index].set(col_pushed).reshape(experts, sources * CAP, FEATS)

    def per_region(bundle):
        return closure_pass(bundle[0], bundle[1], bundle[2], bundle[3], bundle[4])

    raw_tend, back_in, grad_in, grad_mid, grad_out = lax.map(per_region, (buffer_in, buffer_pushed, w_in, w_mid, w_out))
    tend_grid = from_blocks(raw_tend.reshape(-1, FEATS)[slot_index])
    back_grid = from_blocks(back_in.reshape(-1, FEATS)[slot_index])
    tendency = (active[None] * tend_grid.astype(jnp.float32)).astype(jnp.bfloat16)
    state_grad = cotangent + back_grid.astype(jnp.float32)
    for number in range(STEPS):
        state_grad = retreat_whole(state_grad, coefficients)
    return advected, tendency, state_grad, grad_in, grad_mid, grad_out
```

```python
import functools

import jax
import jax.numpy as jnp
from jax import lax
from jax.experimental import pallas as pl
from jax.experimental.pallas import tpu as pltpu
from jax.sharding import PartitionSpec as P

STEPS = 2


def padded_2(value, sides, width, wrap):
    for axis, dim in sides:
        size, length = (lax.axis_size(axis), value.shape[dim])
        up = [(i, (i + 1) % size) for i in range(size if wrap else size - 1)]
        down = [(j, i) for i, j in up]
        last = lax.slice_in_dim(value, length - width, length, axis=dim)
        leading = lax.slice_in_dim(value, 0, width, axis=dim)
        before = lax.ppermute(last, axis, up)
        after = lax.ppermute(leading, axis, down)
        value = jnp.concatenate([before, value, after], axis=dim)
    return value


def build_table(diffusivity, east_peclet, north_peclet, sea_mask, depth_levels):
    levels = lax.broadcasted_iota(jnp.int32, diffusivity.shape, 0)
    active = (levels < depth_levels[None]).astype(jnp.float32) * sea_mask[None].astype(jnp.float32)
    return jnp.stack(
        [
            diffusivity * (1.0 - east_peclet),
            diffusivity * (1.0 + east_peclet),
            diffusivity * (1.0 - north_peclet),
            diffusivity * (1.0 + north_peclet),
            4.0 * diffusivity,
            active,
        ]
    )


def with_rims(grid_values, width):
    padded = padded_2(grid_values, (("lat", 2),), width, False)
    return padded_2(padded, ((("lon", "cl"), 3),), width, True)


def advance(padded, coefficients):
    inner_coef = coefficients[:, :, 1:-1, 1:-1]
    interior = padded[:, :, 1:-1, 1:-1]
    change = inner_coef[0] * padded[:, :, 1:-1, 2:] + inner_coef[1] * padded[:, :, 1:-1, :-2]
    change = (
        change + inner_coef[2] * padded[:, :, 2:, 1:-1] + inner_coef[3] * padded[:, :, :-2, 1:-1]
    )
    return interior + inner_coef[5] * (change - inner_coef[4] * interior)


def retreat(padded, coefficients):
    pushed = coefficients[5] * padded
    summed = padded[:, :, 1:-1, 1:-1] - (coefficients[4] * pushed)[:, :, 1:-1, 1:-1]
    summed = (
        summed
        + (coefficients[0] * pushed)[:, :, 1:-1, :-2]
        + (coefficients[1] * pushed)[:, :, 1:-1, 2:]
    )
    summed = (
        summed
        + (coefficients[2] * pushed)[:, :, :-2, 1:-1]
        + (coefficients[3] * pushed)[:, :, 2:, 1:-1]
    )
    return summed


def sweep_steps(grid_values, coefficients, update):
    for number in range(STEPS):
        grid_values = update(with_rims(grid_values, 1), coefficients)
    return grid_values


def project(left, right):
    return jnp.dot(left, right, preferred_element_type=jnp.float32)


def project_back(left, right):
    return lax.dot_general(
        left, right, (((1,), (1,)), ((), ())), preferred_element_type=jnp.float32
    )


def contract_rows(left, right):
    return lax.dot_general(
        left, right, (((0,), (0,)), ((), ())), preferred_element_type=jnp.float32
    )


def closure_pass(inputs, pushed, w_in, w_mid, w_out):
    slopes = []
    layers = [inputs]
    shaped = jnp.tanh(project(inputs, w_in))
    slopes.append(1.0 - shaped * shaped)
    acting = shaped.astype(jnp.bfloat16)
    layers.append(acting)
    layer_index = 0
    shaped = jnp.tanh(project(acting, w_mid[layer_index]))
    slopes.append(1.0 - shaped * shaped)
    acting = shaped.astype(jnp.bfloat16)
    layers.append(acting)
    raw_tend = project(acting, w_out).astype(jnp.bfloat16)
    grad_out = contract_rows(acting, pushed)
    backward = project_back(pushed, w_out)
    mid_grads = []
    for layer_index in reversed(range(w_mid.shape[0])):
        deltas = (backward * slopes[layer_index + 1]).astype(jnp.bfloat16)
        mid_grads.append(contract_rows(layers[layer_index + 1], deltas))
        backward = project_back(deltas, w_mid[layer_index])
    deltas = (backward * slopes[0]).astype(jnp.bfloat16)
    grad_in = contract_rows(inputs, deltas)
    back_in = project_back(deltas, w_in).astype(jnp.bfloat16)
    return (raw_tend, back_in, grad_in, jnp.stack(mid_grads[::-1]), grad_out)


def on_device(
    ocean_state,
    cotangent,
    diffusivity,
    east_peclet,
    north_peclet,
    sea_mask,
    depth_levels,
    owner_table,
    w_in,
    w_mid,
    w_out,
):
    coefficients = build_table(diffusivity, east_peclet, north_peclet, sea_mask, depth_levels)
    active = coefficients[5]
    rim_width = 1
    coef_rims = with_rims(coefficients, rim_width)
    advected = sweep_steps(ocean_state, coef_rims, advance)
    features = ocean_state.shape[0] * ocean_state.shape[1]
    columns = ocean_state.shape[2] * ocean_state.shape[3]
    experts = lax.axis_size(("lon", "lat"))
    capacity = 2 * columns // experts
    owners = owner_table.reshape(columns)
    one_hot = (owners[:, None] == lax.broadcasted_iota(jnp.int32, (columns, experts), 1)).astype(
        jnp.int32
    )
    rank_in = jnp.sum(jnp.cumsum(one_hot, axis=0) * one_hot, axis=1) - 1
    slot_index = owners * capacity + rank_in
    col_inputs = advected.reshape(features, columns).T.astype(jnp.bfloat16)
    col_pushed = (active[None] * cotangent).reshape(features, columns).T.astype(jnp.bfloat16)
    empty = jnp.zeros((experts * capacity, features), jnp.bfloat16)
    send_inputs = empty.at[slot_index].set(col_inputs)
    send_pushed = empty.at[slot_index].set(col_pushed)
    got_inputs, got_pushed = (
        lax.all_to_all(send_inputs, ("lon", "lat"), split_axis=0, concat_axis=0, tiled=True),
        lax.all_to_all(send_pushed, ("lon", "lat"), split_axis=0, concat_axis=0, tiled=True),
    )
    raw_tend, back_in, grad_in, grad_mid, grad_out = closure_pass(
        got_inputs, got_pushed, w_in[0], w_mid[0], w_out[0]
    )
    grad_in, grad_mid, grad_out = lax.psum((grad_in, grad_mid, grad_out), "cl")
    ret_tend, ret_back = (
        lax.all_to_all(raw_tend, ("lon", "lat"), split_axis=0, concat_axis=0, tiled=True),
        lax.all_to_all(back_in, ("lon", "lat"), split_axis=0, concat_axis=0, tiled=True),
    )
    tend_grid = ret_tend[slot_index].T.reshape(ocean_state.shape)
    back_grid = ret_back[slot_index].T.reshape(ocean_state.shape)
    tendency = (active[None] * tend_grid.astype(jnp.float32)).astype(jnp.bfloat16)
    adjoint_start = cotangent + back_grid.astype(jnp.float32)
    state_grad = sweep_steps(adjoint_start, coef_rims, retreat)
    return (advected, tendency, state_grad, grad_in[None], grad_mid[None], grad_out[None])


MESH = pl.DeviceIdType.MESH
VMEM_BYTES = 48 * 1024 * 1024


def matmul(left, right, contract):
    return lax.dot_general(
        left, right, (((contract[0],), (contract[1],)), ((), ())),
        preferred_element_type=jnp.float32,
    )


def tile_kernel(
    n_lon, n_lat, n_cl, cap,
    x_ref, cot_ref, diff_ref, ep_ref, np_ref, sea_ref, dep_ref, own_ref, wi_ref, wm_ref, wo_ref,
    adv_ref, tend_ref, sg_ref, gi_ref, gm_ref, go_ref,
    d8, tmp, hal, lat_s, lat_r, lon_s, lon_r, pt, snd, rcv, gis, gms, gos, gir, gmr, gor,
    lat_ss, lat_rs, lon_ss, lon_rs, a2a_ss, a2a_rs, g_ss, g_rs,
):
    experts = n_lon * n_lat
    lon, lat, cl = lax.axis_index("lon"), lax.axis_index("lat"), lax.axis_index("cl")
    ring = n_lon * n_cl
    place = lon * n_cl + cl
    east, west = (place + 1) % ring, (place + ring - 1) % ring
    east_id = {"lon": east // n_cl, "cl": east % n_cl}
    west_id = {"lon": west // n_cl, "cl": west % n_cl}
    lat_id = {"lat": 1 - lat}
    cl_id = {"cl": 1 - cl}
    me = lon * n_lat + lat
    partners = [(me + d) % experts for d in range(experts)]
    partner_ids = [{"lon": p // n_lat, "lat": p % n_lat} for p in partners]

    barrier = pltpu.get_barrier_semaphore()
    for other in partner_ids[1:] + [east_id, west_id]:
        pl.semaphore_signal(barrier, inc=1, device_id=other, device_id_type=MESH)

    rows, wide = x_ref.shape
    tiles = rows // 8
    fields = rows // diff_ref.shape[0]
    feats = rows // 4
    cube = (tiles, 8, wide)
    four = (fields, tiles // fields, 8, wide)
    lane = lax.broadcasted_iota(jnp.int32, cube, 2)
    tile = lax.broadcasted_iota(jnp.int32, cube, 0)
    row = lax.broadcasted_iota(jnp.int32, cube, 1) % 4
    on_tile = lane == tile
    south = jnp.full(cube, lat, jnp.int32) == 0

    d8[0, 0:4], d8[0, 4:8] = sea_ref[...], sea_ref[...]
    d8[1, 0:4], d8[1, 4:8] = dep_ref[...], dep_ref[...]
    flat = (tiles // fields, 8, wide)
    level = 2 * lax.broadcasted_iota(jnp.int32, flat, 0) + (
        lax.broadcasted_iota(jnp.int32, flat, 1) // 4
    )
    diff = diff_ref[...].reshape(flat)
    ep, np_ = ep_ref[...].reshape(flat), np_ref[...].reshape(flat)
    active = (level < d8[1][None]).astype(jnp.float32) * d8[0][None].astype(jnp.float32)
    c_e, c_w = (diff * (1.0 - ep))[None], (diff * (1.0 + ep))[None]
    c_n, c_s = (diff * (1.0 - np_))[None], (diff * (1.0 + np_))[None]
    c_0, act = (4.0 * diff)[None], active[None]

    def pack(value, side):
        return jnp.sum(jnp.where(on_tile, value[:, :, side : side + 1], 0.0), axis=0)

    def unpack(packed):
        return jnp.sum(jnp.where(on_tile, packed[None], 0.0), axis=2, keepdims=True)

    def send_edges(number, to_e, to_w, to_n, to_s):
        tmp[...] = jnp.where(south, to_n, to_s).reshape(rows, wide)
        pick = jnp.full((feats, wide), lat, jnp.int32) == 0
        lat_s[number] = jnp.where(
            pick, tmp[pl.ds(3, feats, stride=4), :], tmp[pl.ds(0, feats, stride=4), :]
        )
        lon_s[number, 0] = pack(to_e, wide - 1)
        lon_s[number, 1] = pack(to_w, 0)
        copies = [
            pltpu.make_async_remote_copy(
                lat_s.at[number], lat_r.at[number], lat_ss.at[number], lat_rs.at[number],
                device_id=lat_id, device_id_type=MESH,
            ),
            pltpu.make_async_remote_copy(
                lon_s.at[number, 0], lon_r.at[number, 0],
                lon_ss.at[number, 0], lon_rs.at[number, 0],
                device_id=east_id, device_id_type=MESH,
            ),
            pltpu.make_async_remote_copy(
                lon_s.at[number, 1], lon_r.at[number, 1],
                lon_ss.at[number, 1], lon_rs.at[number, 1],
                device_id=west_id, device_id_type=MESH,
            ),
        ]
        for copy in copies:
            copy.start()
        return copies

    def shifted(number, copies, to_e, to_w, to_n, to_s):
        for copy in copies:
            copy.wait()
        from_w = jnp.where(lane == 0, unpack(lon_r[number, 0]), pltpu.roll(to_e, 1, 2))
        from_e = jnp.where(
            lane == wide - 1, unpack(lon_r[number, 1]), pltpu.roll(to_w, wide - 1, 2)
        )
        hal[pl.ds(0, feats, stride=4), :] = lat_r[number]
        hal[pl.ds(3, feats, stride=4), :] = lat_r[number]
        edge = hal[...].reshape(cube)
        from_s = jnp.where(row == 0, jnp.where(south, 0.0, edge), pltpu.roll(to_n, 1, 1))
        from_n = jnp.where(row == 3, jnp.where(south, edge, 0.0), pltpu.roll(to_s, 7, 1))
        return [v.reshape(four) for v in (from_w, from_e, from_s, from_n)]

    def exchange(kind):
        copies = []
        for d in range(1, experts):
            copies.append(
                pltpu.make_async_remote_copy(
                    snd.at[kind, partners[d]], rcv.at[kind, me],
                    a2a_ss.at[kind, d], a2a_rs.at[kind, d],
                    device_id=partner_ids[d], device_id_type=MESH,
                )
            )
            copies[-1].start()
        rcv[kind, me] = snd[kind, me]
        return copies

    def arrived(kind, copies):
        for copy in copies:
            copy.wait()
        return jnp.concatenate([rcv[kind, e] for e in range(experts)], axis=1)

    def columns_of(ref):
        return jnp.concatenate(
            [ref[pl.ds(i, feats, stride=4), :] for i in range(4)], axis=1
        ).astype(jnp.bfloat16)

    def to_slots(kind, columns):
        slots = matmul(columns, pt[...], (1, 1)).astype(jnp.bfloat16)
        for e in range(experts):
            snd[kind, e] = slots[:, e * cap : (e + 1) * cap]

    def to_grid(slots):
        columns = matmul(slots, pt[...], (1, 0))
        for i in range(4):
            tmp[pl.ds(i, feats, stride=4), :] = columns[:, i * wide : (i + 1) * wide]
        return tmp[...].reshape(four)

    count = 4 * wide
    owners = jnp.concatenate([own_ref[i : i + 1, :] for i in range(4)], axis=1)
    hot = (owners == lax.broadcasted_iota(jnp.int32, (experts, count), 0)).astype(jnp.float32)
    before = (
        lax.broadcasted_iota(jnp.int32, (count, count), 0)
        < lax.broadcasted_iota(jnp.int32, (count, count), 1)
    ).astype(jnp.float32).astype(jnp.bfloat16)
    earlier = matmul(hot.astype(jnp.bfloat16), before, (1, 0))
    rank = jnp.sum(hot * earlier, axis=0, keepdims=True)
    slot = owners * cap + rank.astype(jnp.int32)
    pt[...] = (
        lax.broadcasted_iota(jnp.int32, (experts * cap, count), 0) == slot
    ).astype(jnp.float32).astype(jnp.bfloat16)

    cot = cot_ref[...].reshape(four)
    tmp[...] = (act * cot).reshape(rows, wide)
    to_slots(0, columns_of(tmp))

    pl.semaphore_wait(barrier, experts - 1 + 2)

    state = x_ref[...].reshape(four)
    sent = []
    for number in range(STEPS):
        whole = state.reshape(cube)
        copies = send_edges(number, whole, whole, whole, whole)
        if number == 0:
            sent = exchange(0)
        from_w, from_e, from_s, from_n = shifted(number, copies, whole, whole, whole, whole)
        change = c_e * from_e + c_w * from_w + c_n * from_n + c_s * from_s
        state = state + act * (change - c_0 * state)
    adv_ref[...] = state.reshape(rows, wide)
    to_slots(1, columns_of(adv_ref))
    sent_in = exchange(1)
    pushed = arrived(0, sent)
    back_2 = matmul(wo_ref[...], pushed, (1, 0))
    inputs = arrived(1, sent_in)

    t_0 = jnp.tanh(matmul(wi_ref[...], inputs, (0, 0)))
    a_0 = t_0.astype(jnp.bfloat16)
    t_1 = jnp.tanh(matmul(wm_ref[...], a_0, (0, 0)))
    a_1 = t_1.astype(jnp.bfloat16)
    delta_1 = (back_2 * (1.0 - t_1 * t_1)).astype(jnp.bfloat16)
    back_1 = matmul(wm_ref[...], delta_1, (1, 0))
    delta_0 = (back_1 * (1.0 - t_0 * t_0)).astype(jnp.bfloat16)
    back_in = matmul(wi_ref[...], delta_0, (1, 0)).astype(jnp.bfloat16)
    for e in range(experts):
        snd[2, e] = back_in[:, e * cap : (e + 1) * cap]
    sent_back = exchange(2)
    raw = matmul(wo_ref[...], a_1, (0, 0)).astype(jnp.bfloat16)
    for e in range(experts):
        snd[3, e] = raw[:, e * cap : (e + 1) * cap]
    sent_raw = exchange(3)
    gis[...] = matmul(inputs, delta_0, (1, 1))
    gms[...] = matmul(a_0, delta_1, (1, 1))
    gos[...] = matmul(a_1, pushed, (1, 1))
    sent_grads = []
    for i, (src, dst) in enumerate(((gis, gir), (gms, gmr), (gos, gor))):
        sent_grads.append(
            pltpu.make_async_remote_copy(
                src, dst, g_ss.at[i], g_rs.at[i], device_id=cl_id, device_id_type=MESH
            )
        )
        sent_grads[-1].start()

    grad = cot + to_grid(arrived(2, sent_back))
    for number in range(STEPS, 2 * STEPS):
        held = act * grad
        parts = [(c * held).reshape(cube) for c in (c_e, c_w, c_n, c_s)]
        copies = send_edges(number, *parts)
        base = grad - c_0 * held
        if number == 2 * STEPS - 1:
            tend = arrived(3, sent_raw)
        from_w, from_e, from_s, from_n = shifted(number, copies, *parts)
        grad = base + from_w + from_e + from_s + from_n
    sg_ref[...] = grad.reshape(rows, wide)
    tend_ref[...] = (act * to_grid(tend)).reshape(rows, wide)
    for copy in sent_grads:
        copy.wait()
    gi_ref[...] = gis[...] + gir[...]
    gm_ref[...] = gms[...] + gmr[...]
    go_ref[...] = gos[...] + gor[...]


def on_device_fused(
    ocean_state, cotangent, diffusivity, east_peclet, north_peclet, sea_mask, depth_levels,
    owner_table, w_in, w_mid, w_out,
):
    n_lon, n_lat, n_cl = (lax.axis_size(axis) for axis in ("lon", "lat", "cl"))
    wide = ocean_state.shape[3]
    rows = ocean_state.size // wide
    columns = 4 * wide
    experts = n_lon * n_lat
    cap = 2 * columns // experts
    feats, hidden = w_in.shape[1:]
    f32, bf16 = jnp.float32, jnp.bfloat16
    vmem = pl.BlockSpec(memory_space=pltpu.VMEM)
    flat = lambda v: v.reshape(-1, wide)
    out = pl.pallas_call(
        functools.partial(tile_kernel, n_lon, n_lat, n_cl, cap),
        out_shape=[
            jax.ShapeDtypeStruct((rows, wide), f32),
            jax.ShapeDtypeStruct((rows, wide), f32),
            jax.ShapeDtypeStruct((rows, wide), f32),
            jax.ShapeDtypeStruct((feats, hidden), f32),
            jax.ShapeDtypeStruct((hidden, hidden), f32),
            jax.ShapeDtypeStruct((hidden, feats), f32),
        ],
        in_specs=[vmem] * 11,
        out_specs=[vmem] * 6,
        scratch_shapes=[
            pltpu.VMEM((2, 8, wide), jnp.int32),
            pltpu.VMEM((rows, wide), f32),
            pltpu.VMEM((rows, wide), f32),
            pltpu.VMEM((2 * STEPS, feats, wide), f32),
            pltpu.VMEM((2 * STEPS, feats, wide), f32),
            pltpu.VMEM((2 * STEPS, 2, 8, wide), f32),
            pltpu.VMEM((2 * STEPS, 2, 8, wide), f32),
            pltpu.VMEM((experts * cap, columns), bf16),
            pltpu.VMEM((4, experts, feats, cap), bf16),
            pltpu.VMEM((4, experts, feats, cap), bf16),
        ]
        + [pltpu.VMEM(s, f32) for s in ((feats, hidden), (hidden, hidden), (hidden, feats))] * 2
        + [pltpu.SemaphoreType.DMA((2 * STEPS,))] * 2
        + [pltpu.SemaphoreType.DMA((2 * STEPS, 2))] * 2
        + [pltpu.SemaphoreType.DMA((4, experts))] * 2
        + [pltpu.SemaphoreType.DMA((3,))] * 2,
        compiler_params=pltpu.CompilerParams(
            collective_id=0, has_side_effects=True, vmem_limit_bytes=VMEM_BYTES
        ),
    )(
        flat(ocean_state), flat(cotangent), flat(diffusivity), flat(east_peclet),
        flat(north_peclet), sea_mask, depth_levels, flat(owner_table), w_in[0], w_mid[0, 0],
        w_out[0],
    )
    advected, tendency, state_grad, grad_in, grad_mid, grad_out = out
    shape = ocean_state.shape
    return (
        advected.reshape(shape), tendency.astype(bf16).reshape(shape), state_grad.reshape(shape),
        grad_in[None], grad_mid[None, None], grad_out[None],
    )


def solution(mesh):
    few = mesh.shape["lat"] == 2 and mesh.shape["cl"] == 2 and 2 < mesh.shape["lon"] <= 4
    plan = on_device_fused if few else on_device
    return jax.shard_map(
        plan,
        mesh=mesh,
        in_specs=(
            P("groups", None, "lat", ("lon", "cl")),
            P("groups", None, "lat", ("lon", "cl")),
            P(None, "lat", ("lon", "cl")),
            P(None, "lat", ("lon", "cl")),
            P(None, "lat", ("lon", "cl")),
            P("lat", ("lon", "cl")),
            P("lat", ("lon", "cl")),
            P("lat", ("lon", "cl"), None, None),
            P(("lon", "lat"), None, None),
            P(("lon", "lat"), None, None, None),
            P(("lon", "lat"), None, None),
        ),
        out_specs=(
            P("groups", None, "lat", ("lon", "cl")),
            P("groups", None, "lat", ("lon", "cl")),
            P("groups", None, "lat", ("lon", "cl")),
            P(("groups", "lon", "lat"), None, None),
            P(("groups", "lon", "lat"), None, None, None),
            P(("groups", "lon", "lat"), None, None),
        ),
        check_vma=False,
    )
```

```python
import functools

import jax
import jax.numpy as jnp
from jax import lax
from jax.experimental import pallas as pl
from jax.experimental.pallas import tpu as pltpu
from jax.sharding import PartitionSpec as P

STEPS = 2


def padded_2(value, sides, width, wrap):
    for axis, dim in sides:
        size, length = (lax.axis_size(axis), value.shape[dim])
        up = [(i, (i + 1) % size) for i in range(size if wrap else size - 1)]
        down = [(j, i) for i, j in up]
        last = lax.slice_in_dim(value, length - width, length, axis=dim)
        leading = lax.slice_in_dim(value, 0, width, axis=dim)
        before = lax.ppermute(last, axis, up)
        after = lax.ppermute(leading, axis, down)
        value = jnp.concatenate([before, value, after], axis=dim)
    return value


def build_table(diffusivity, east_peclet, north_peclet, sea_mask, depth_levels):
    levels = lax.broadcasted_iota(jnp.int32, diffusivity.shape, 0)
    active = (levels < depth_levels[None]).astype(jnp.float32) * sea_mask[None].astype(jnp.float32)
    return jnp.stack(
        [
            diffusivity * (1.0 - east_peclet),
            diffusivity * (1.0 + east_peclet),
            diffusivity * (1.0 - north_peclet),
            diffusivity * (1.0 + north_peclet),
            4.0 * diffusivity,
            active,
        ]
    )


def with_rims(grid_values, width):
    padded = padded_2(grid_values, (("lat", 2),), width, False)
    return padded_2(padded, ((("lon", "cl"), 3),), width, True)


def advance(padded, coefficients):
    inner_coef = coefficients[:, :, 1:-1, 1:-1]
    interior = padded[:, :, 1:-1, 1:-1]
    change = inner_coef[0] * padded[:, :, 1:-1, 2:] + inner_coef[1] * padded[:, :, 1:-1, :-2]
    change = (
        change + inner_coef[2] * padded[:, :, 2:, 1:-1] + inner_coef[3] * padded[:, :, :-2, 1:-1]
    )
    return interior + inner_coef[5] * (change - inner_coef[4] * interior)


def retreat(padded, coefficients):
    pushed = coefficients[5] * padded
    summed = padded[:, :, 1:-1, 1:-1] - (coefficients[4] * pushed)[:, :, 1:-1, 1:-1]
    summed = (
        summed
        + (coefficients[0] * pushed)[:, :, 1:-1, :-2]
        + (coefficients[1] * pushed)[:, :, 1:-1, 2:]
    )
    summed = (
        summed
        + (coefficients[2] * pushed)[:, :, :-2, 1:-1]
        + (coefficients[3] * pushed)[:, :, 2:, 1:-1]
    )
    return summed


def sweep_steps(grid_values, coefficients, update):
    for number in range(STEPS):
        grid_values = update(with_rims(grid_values, 1), coefficients)
    return grid_values


def project(left, right):
    return jnp.dot(left, right, preferred_element_type=jnp.float32)


def project_back(left, right):
    return lax.dot_general(
        left, right, (((1,), (1,)), ((), ())), preferred_element_type=jnp.float32
    )


def contract_rows(left, right):
    return lax.dot_general(
        left, right, (((0,), (0,)), ((), ())), preferred_element_type=jnp.float32
    )


def closure_pass(inputs, pushed, w_in, w_mid, w_out):
    slopes = []
    layers = [inputs]
    shaped = jnp.tanh(project(inputs, w_in))
    slopes.append(1.0 - shaped * shaped)
    acting = shaped.astype(jnp.bfloat16)
    layers.append(acting)
    layer_index = 0
    shaped = jnp.tanh(project(acting, w_mid[layer_index]))
    slopes.append(1.0 - shaped * shaped)
    acting = shaped.astype(jnp.bfloat16)
    layers.append(acting)
    raw_tend = project(acting, w_out).astype(jnp.bfloat16)
    grad_out = contract_rows(acting, pushed)
    backward = project_back(pushed, w_out)
    mid_grads = []
    for layer_index in reversed(range(w_mid.shape[0])):
        deltas = (backward * slopes[layer_index + 1]).astype(jnp.bfloat16)
        mid_grads.append(contract_rows(layers[layer_index + 1], deltas))
        backward = project_back(deltas, w_mid[layer_index])
    deltas = (backward * slopes[0]).astype(jnp.bfloat16)
    grad_in = contract_rows(inputs, deltas)
    back_in = project_back(deltas, w_in).astype(jnp.bfloat16)
    return (raw_tend, back_in, grad_in, jnp.stack(mid_grads[::-1]), grad_out)


def on_device(
    ocean_state,
    cotangent,
    diffusivity,
    east_peclet,
    north_peclet,
    sea_mask,
    depth_levels,
    owner_table,
    w_in,
    w_mid,
    w_out,
):
    coefficients = build_table(diffusivity, east_peclet, north_peclet, sea_mask, depth_levels)
    active = coefficients[5]
    rim_width = 1
    coef_rims = with_rims(coefficients, rim_width)
    advected = sweep_steps(ocean_state, coef_rims, advance)
    features = ocean_state.shape[0] * ocean_state.shape[1]
    columns = ocean_state.shape[2] * ocean_state.shape[3]
    experts = lax.axis_size(("lon", "lat"))
    capacity = 2 * columns // experts
    owners = owner_table.reshape(columns)
    one_hot = (owners[:, None] == lax.broadcasted_iota(jnp.int32, (columns, experts), 1)).astype(
        jnp.int32
    )
    rank_in = jnp.sum(jnp.cumsum(one_hot, axis=0) * one_hot, axis=1) - 1
    slot_index = owners * capacity + rank_in
    col_inputs = advected.reshape(features, columns).T.astype(jnp.bfloat16)
    col_pushed = (active[None] * cotangent).reshape(features, columns).T.astype(jnp.bfloat16)
    empty = jnp.zeros((experts * capacity, features), jnp.bfloat16)
    send_inputs = empty.at[slot_index].set(col_inputs)
    send_pushed = empty.at[slot_index].set(col_pushed)
    got_inputs, got_pushed = (
        lax.all_to_all(send_inputs, ("lon", "lat"), split_axis=0, concat_axis=0, tiled=True),
        lax.all_to_all(send_pushed, ("lon", "lat"), split_axis=0, concat_axis=0, tiled=True),
    )
    raw_tend, back_in, grad_in, grad_mid, grad_out = closure_pass(
        got_inputs, got_pushed, w_in[0], w_mid[0], w_out[0]
    )
    grad_in, grad_mid, grad_out = lax.psum((grad_in, grad_mid, grad_out), "cl")
    ret_tend, ret_back = (
        lax.all_to_all(raw_tend, ("lon", "lat"), split_axis=0, concat_axis=0, tiled=True),
        lax.all_to_all(back_in, ("lon", "lat"), split_axis=0, concat_axis=0, tiled=True),
    )
    tend_grid = ret_tend[slot_index].T.reshape(ocean_state.shape)
    back_grid = ret_back[slot_index].T.reshape(ocean_state.shape)
    tendency = (active[None] * tend_grid.astype(jnp.float32)).astype(jnp.bfloat16)
    adjoint_start = cotangent + back_grid.astype(jnp.float32)
    state_grad = sweep_steps(adjoint_start, coef_rims, retreat)
    return (advected, tendency, state_grad, grad_in[None], grad_mid[None], grad_out[None])


MESH = pl.DeviceIdType.MESH
VMEM_BYTES = 61 * 1024 * 1024


def matmul(left, right, contract):
    return lax.dot_general(
        left, right, (((contract[0],), (contract[1],)), ((), ())),
        preferred_element_type=jnp.float32,
    )


def tile_kernel(
    n_lon, n_lat, n_cl, cap,
    x_hbm, cot_hbm, diff_hbm, ep_hbm, np_hbm, sea_hbm, dep_hbm, own_hbm, wi_hbm, wm_hbm, wo_hbm,
    adv_hbm, tend_hbm, sg_hbm, gi_hbm, gm_hbm, go_hbm,
    x_ref, cot_ref, diff_ref, ep_ref, np_ref, sea_ref, dep_ref, own_ref, wi_ref, wm_ref, wo_ref,
    adv_ref, tend_ref, sg_ref, gi_ref, gm_ref, go_ref, load_sem, store_sem, d8, tmp, hal, lat_s, lat_r, lon_s, lon_r, pt, snd, rcv, gis, gms, gos, gir, gmr, gor,
    lat_ss, lat_rs, lon_ss, lon_rs, a2a_ss, a2a_rs, g_ss, g_rs,
):
    experts = n_lon * n_lat
    lon, lat, cl = lax.axis_index("lon"), lax.axis_index("lat"), lax.axis_index("cl")
    ring = n_lon * n_cl
    place = lon * n_cl + cl
    east, west = (place + 1) % ring, (place + ring - 1) % ring
    east_id = {"lon": east // n_cl, "cl": east % n_cl}
    west_id = {"lon": west // n_cl, "cl": west % n_cl}
    lat_id = {"lat": 1 - lat}
    cl_id = {"cl": 1 - cl}
    me = lon * n_lat + lat
    partners = [(me + d) % experts for d in range(experts)]
    partner_ids = [{"lon": p // n_lat, "lat": p % n_lat} for p in partners]

    barrier = pltpu.get_barrier_semaphore()
    for other in partner_ids[1:] + [east_id, west_id]:
        pl.semaphore_signal(barrier, inc=1, device_id=other, device_id_type=MESH)

    loads = {}
    for i, (name, src, dst) in enumerate((
        ("x", x_hbm, x_ref), ("diff", diff_hbm, diff_ref), ("ep", ep_hbm, ep_ref),
        ("np", np_hbm, np_ref), ("sea", sea_hbm, sea_ref), ("dep", dep_hbm, dep_ref),
        ("own", own_hbm, own_ref), ("cot", cot_hbm, cot_ref), ("wo", wo_hbm, wo_ref),
        ("wi", wi_hbm, wi_ref), ("wm", wm_hbm, wm_ref),
    )):
        loads[name] = pltpu.make_async_copy(src, dst, load_sem.at[i])
        loads[name].start()

    results = (
        (adv_ref, adv_hbm), (tend_ref, tend_hbm), (sg_ref, sg_hbm),
        (gi_ref, gi_hbm), (gm_ref, gm_hbm), (go_ref, go_hbm),
    )
    stores = [
        pltpu.make_async_copy(a, b, store_sem.at[i]) for i, (a, b) in enumerate(results)
    ]

    rows, wide = x_ref.shape
    tiles = rows // 8
    fields = rows // diff_ref.shape[0]
    feats = rows // 4
    cube = (tiles, 8, wide)
    four = (fields, tiles // fields, 8, wide)
    lane = lax.broadcasted_iota(jnp.int32, cube, 2)
    tile = lax.broadcasted_iota(jnp.int32, cube, 0)
    row = lax.broadcasted_iota(jnp.int32, cube, 1) % 4
    on_tile = lane == tile
    south = jnp.full(cube, lat, jnp.int32) == 0

    for name in ("sea", "dep", "diff", "ep", "np"):
        loads[name].wait()
    d8[0, 0:4], d8[0, 4:8] = sea_ref[...], sea_ref[...]
    d8[1, 0:4], d8[1, 4:8] = dep_ref[...], dep_ref[...]
    flat = (tiles // fields, 8, wide)
    level = 2 * lax.broadcasted_iota(jnp.int32, flat, 0) + (
        lax.broadcasted_iota(jnp.int32, flat, 1) // 4
    )
    diff = diff_ref[...].reshape(flat)
    ep, np_ = ep_ref[...].reshape(flat), np_ref[...].reshape(flat)
    active = (level < d8[1][None]).astype(jnp.float32) * d8[0][None].astype(jnp.float32)
    c_e, c_w = (diff * (1.0 - ep))[None], (diff * (1.0 + ep))[None]
    c_n, c_s = (diff * (1.0 - np_))[None], (diff * (1.0 + np_))[None]
    c_0, act = (4.0 * diff)[None], active[None]

    def pack(value, side):
        return jnp.sum(jnp.where(on_tile, value[:, :, side : side + 1], 0.0), axis=0)

    def unpack(packed):
        return jnp.sum(jnp.where(on_tile, packed[None], 0.0), axis=2, keepdims=True)

    def send_edges(number, to_e, to_w, to_n, to_s):
        tmp[...] = jnp.where(south, to_n, to_s).reshape(rows, wide)
        pick = jnp.full((feats, wide), lat, jnp.int32) == 0
        lat_s[number] = jnp.where(
            pick, tmp[pl.ds(3, feats, stride=4), :], tmp[pl.ds(0, feats, stride=4), :]
        ).astype(jnp.bfloat16)
        lon_s[number, 0] = pack(to_e, wide - 1)
        lon_s[number, 1] = pack(to_w, 0)
        copies = [
            pltpu.make_async_remote_copy(
                lat_s.at[number], lat_r.at[number], lat_ss.at[number], lat_rs.at[number],
                device_id=lat_id, device_id_type=MESH,
            ),
            pltpu.make_async_remote_copy(
                lon_s.at[number, 0], lon_r.at[number, 0],
                lon_ss.at[number, 0], lon_rs.at[number, 0],
                device_id=east_id, device_id_type=MESH,
            ),
            pltpu.make_async_remote_copy(
                lon_s.at[number, 1], lon_r.at[number, 1],
                lon_ss.at[number, 1], lon_rs.at[number, 1],
                device_id=west_id, device_id_type=MESH,
            ),
        ]
        for copy in copies:
            copy.start()
        return copies

    def shifted(number, copies, to_e, to_w, to_n, to_s):
        for copy in copies:
            copy.wait()
        from_w = jnp.where(lane == 0, unpack(lon_r[number, 0]), pltpu.roll(to_e, 1, 2))
        from_e = jnp.where(
            lane == wide - 1, unpack(lon_r[number, 1]), pltpu.roll(to_w, wide - 1, 2)
        )
        beyond = lat_r[number].astype(jnp.float32)
        hal[pl.ds(0, feats, stride=4), :] = beyond
        hal[pl.ds(3, feats, stride=4), :] = beyond
        edge = hal[...].reshape(cube)
        from_s = jnp.where(row == 0, jnp.where(south, 0.0, edge), pltpu.roll(to_n, 1, 1))
        from_n = jnp.where(row == 3, jnp.where(south, edge, 0.0), pltpu.roll(to_s, 7, 1))
        return [v.reshape(four) for v in (from_w, from_e, from_s, from_n)]

    def exchange(kind):
        copies = []
        for d in range(1, experts):
            copies.append(
                pltpu.make_async_remote_copy(
                    snd.at[kind, partners[d]], rcv.at[kind, me],
                    a2a_ss.at[kind, d], a2a_rs.at[kind, d],
                    device_id=partner_ids[d], device_id_type=MESH,
                )
            )
            copies[-1].start()
        rcv[kind, me] = snd[kind, me]
        return copies

    def arrived(kind, copies):
        for copy in copies:
            copy.wait()
        return jnp.concatenate([rcv[kind, e] for e in range(experts)], axis=1)

    def columns_of(ref):
        return jnp.concatenate(
            [ref[pl.ds(i, feats, stride=4), :] for i in range(4)], axis=1
        ).astype(jnp.bfloat16)

    def to_slots(kind, columns):
        slots = matmul(columns, pt[...], (1, 1)).astype(jnp.bfloat16)
        for e in range(experts):
            snd[kind, e] = slots[:, e * cap : (e + 1) * cap]

    def to_grid(slots):
        columns = matmul(slots, pt[...], (1, 0))
        for i in range(4):
            tmp[pl.ds(i, feats, stride=4), :] = columns[:, i * wide : (i + 1) * wide]
        return tmp[...].reshape(four)

    loads["x"].wait()
    state = x_ref[...].reshape(four)
    whole = state.reshape(cube)
    pl.semaphore_wait(barrier, experts - 1 + 2)
    copies = send_edges(0, whole, whole, whole, whole)

    for name in ("own", "cot"):
        loads[name].wait()
    count = 4 * wide
    owners = jnp.concatenate([own_ref[i : i + 1, :] for i in range(4)], axis=1)
    hot = (owners == lax.broadcasted_iota(jnp.int32, (experts, count), 0)).astype(jnp.float32)
    before = (
        lax.broadcasted_iota(jnp.int32, (count, count), 0)
        < lax.broadcasted_iota(jnp.int32, (count, count), 1)
    ).astype(jnp.float32).astype(jnp.bfloat16)
    earlier = matmul(hot.astype(jnp.bfloat16), before, (1, 0))
    rank = jnp.sum(hot * earlier, axis=0, keepdims=True)
    slot = owners * cap + rank.astype(jnp.int32)
    pt[...] = (
        lax.broadcasted_iota(jnp.int32, (experts * cap, count), 0) == slot
    ).astype(jnp.float32).astype(jnp.bfloat16)

    cot = cot_ref[...].reshape(four)
    tmp[...] = (act * cot).reshape(rows, wide)
    to_slots(0, columns_of(tmp))
    sent = exchange(0)

    for number in range(STEPS):
        if number > 0:
            whole = state.reshape(cube)
            copies = send_edges(number, whole, whole, whole, whole)
        from_w, from_e, from_s, from_n = shifted(number, copies, whole, whole, whole, whole)
        change = c_e * from_e + c_w * from_w + c_n * from_n + c_s * from_s
        state = state + act * (change - c_0 * state)
    adv_ref[...] = state.reshape(rows, wide)
    to_slots(1, columns_of(adv_ref))
    sent_in = exchange(1)
    stores[0].start()
    for name in ("wo", "wi", "wm"):
        loads[name].wait()
    pushed = arrived(0, sent)
    back_2 = matmul(wo_ref[...], pushed, (1, 0))
    inputs = arrived(1, sent_in)

    t_0 = jnp.tanh(matmul(wi_ref[...], inputs, (0, 0)))
    a_0 = t_0.astype(jnp.bfloat16)
    t_1 = jnp.tanh(matmul(wm_ref[...], a_0, (0, 0)))
    a_1 = t_1.astype(jnp.bfloat16)
    delta_1 = (back_2 * (1.0 - t_1 * t_1)).astype(jnp.bfloat16)
    back_1 = matmul(wm_ref[...], delta_1, (1, 0))
    delta_0 = (back_1 * (1.0 - t_0 * t_0)).astype(jnp.bfloat16)
    back_in = matmul(wi_ref[...], delta_0, (1, 0)).astype(jnp.bfloat16)
    for e in range(experts):
        snd[2, e] = back_in[:, e * cap : (e + 1) * cap]
    sent_back = exchange(2)
    raw = matmul(wo_ref[...], a_1, (0, 0)).astype(jnp.bfloat16)
    for e in range(experts):
        snd[3, e] = raw[:, e * cap : (e + 1) * cap]
    sent_raw = exchange(3)
    gis[...] = matmul(inputs, delta_0, (1, 1))
    gms[...] = matmul(a_0, delta_1, (1, 1))
    gos[...] = matmul(a_1, pushed, (1, 1))
    sent_grads = []
    for i, (src, dst) in enumerate(((gis, gir), (gms, gmr), (gos, gor))):
        sent_grads.append(
            pltpu.make_async_remote_copy(
                src, dst, g_ss.at[i], g_rs.at[i], device_id=cl_id, device_id_type=MESH
            )
        )
        sent_grads[-1].start()

    grad = cot + to_grid(arrived(2, sent_back))
    for number in range(STEPS, 2 * STEPS):
        held = act * grad
        parts = [(c * held).reshape(cube) for c in (c_e, c_w, c_n, c_s)]
        copies = send_edges(number, *parts)
        base = grad - c_0 * held
        if number == 2 * STEPS - 1:
            tend = arrived(3, sent_raw)
        from_w, from_e, from_s, from_n = shifted(number, copies, *parts)
        grad = base + from_w + from_e + from_s + from_n
    sg_ref[...] = grad.reshape(rows, wide)
    stores[2].start()
    tend_ref[...] = (act * to_grid(tend)).reshape(rows, wide).astype(jnp.bfloat16)
    stores[1].start()
    for copy in sent_grads:
        copy.wait()
    gi_ref[...] = gis[...] + gir[...]
    gm_ref[...] = gms[...] + gmr[...]
    go_ref[...] = gos[...] + gor[...]
    for copy in stores[3:]:
        copy.start()
    for copy in stores:
        copy.wait()


def store_kernel(*refs):
    sem = refs[-1]
    copies = [
        pltpu.make_async_copy(refs[i], refs[i + 6], sem.at[i]) for i in range(6)
    ]
    for copy in copies:
        copy.start()
    for copy in copies:
        copy.wait()


def on_device_fused(
    ocean_state, cotangent, diffusivity, east_peclet, north_peclet, sea_mask, depth_levels,
    owner_table, w_in, w_mid, w_out,
):
    n_lon, n_lat, n_cl = (lax.axis_size(axis) for axis in ("lon", "lat", "cl"))
    wide = ocean_state.shape[3]
    rows = ocean_state.size // wide
    columns = 4 * wide
    experts = n_lon * n_lat
    cap = 2 * columns // experts
    feats, hidden = w_in.shape[1:]
    f32, bf16 = jnp.float32, jnp.bfloat16
    sizes = [(rows, wide)] * 3 + [(feats, hidden), (hidden, hidden), (hidden, feats)]
    results = [
        jax.ShapeDtypeStruct(size, bf16 if i == 1 else f32) for i, size in enumerate(sizes)
    ]
    flat = lambda v: v.reshape(-1, wide)
    hbm = pl.BlockSpec(memory_space=pltpu.HBM)
    operands = (
        flat(ocean_state), flat(cotangent), flat(diffusivity), flat(east_peclet),
        flat(north_peclet), sea_mask, depth_levels, flat(owner_table), w_in[0], w_mid[0, 0],
        w_out[0],
    )
    out = pl.pallas_call(
        functools.partial(tile_kernel, n_lon, n_lat, n_cl, cap),
        out_shape=results,
        in_specs=[hbm] * 11,
        out_specs=[hbm] * 6,
        scratch_shapes=[pltpu.VMEM(v.shape, v.dtype) for v in (*operands, *results)]
        + [
            pltpu.SemaphoreType.DMA((11,)),
            pltpu.SemaphoreType.DMA((6,)),
            pltpu.VMEM((2, 8, wide), jnp.int32),
            pltpu.VMEM((rows, wide), f32),
            pltpu.VMEM((rows, wide), f32),
            pltpu.VMEM((2 * STEPS, feats, wide), bf16),
            pltpu.VMEM((2 * STEPS, feats, wide), bf16),
            pltpu.VMEM((2 * STEPS, 2, 8, wide), f32),
            pltpu.VMEM((2 * STEPS, 2, 8, wide), f32),
            pltpu.VMEM((experts * cap, columns), bf16),
            pltpu.VMEM((4, experts, feats, cap), bf16),
            pltpu.VMEM((4, experts, feats, cap), bf16),
        ]
        + [pltpu.VMEM(s, f32) for s in ((feats, hidden), (hidden, hidden), (hidden, feats))] * 2
        + [pltpu.SemaphoreType.DMA((2 * STEPS,))] * 2
        + [pltpu.SemaphoreType.DMA((2 * STEPS, 2))] * 2
        + [pltpu.SemaphoreType.DMA((4, experts))] * 2
        + [pltpu.SemaphoreType.DMA((3,))] * 2,
        compiler_params=pltpu.CompilerParams(
            collective_id=0, has_side_effects=True, vmem_limit_bytes=VMEM_BYTES
        ),
    )(*operands)
    out = pl.pallas_call(
        store_kernel,
        out_shape=results,
        in_specs=[hbm] * 6,
        out_specs=[hbm] * 6,
        scratch_shapes=[pltpu.SemaphoreType.DMA((6,))],
        compiler_params=pltpu.CompilerParams(vmem_limit_bytes=VMEM_BYTES),
    )(*out)
    advected, tendency, state_grad, grad_in, grad_mid, grad_out = out
    shape = ocean_state.shape
    return (
        advected.reshape(shape), tendency.reshape(shape), state_grad.reshape(shape),
        grad_in[None], grad_mid[None, None], grad_out[None],
    )


def solution(mesh):
    few = mesh.shape["lat"] == 2 and mesh.shape["cl"] == 2 and 2 < mesh.shape["lon"] <= 4
    plan = on_device_fused if few else on_device
    return jax.shard_map(
        plan,
        mesh=mesh,
        in_specs=(
            P("groups", None, "lat", ("lon", "cl")),
            P("groups", None, "lat", ("lon", "cl")),
            P(None, "lat", ("lon", "cl")),
            P(None, "lat", ("lon", "cl")),
            P(None, "lat", ("lon", "cl")),
            P("lat", ("lon", "cl")),
            P("lat", ("lon", "cl")),
            P("lat", ("lon", "cl"), None, None),
            P(("lon", "lat"), None, None),
            P(("lon", "lat"), None, None, None),
            P(("lon", "lat"), None, None),
        ),
        out_specs=(
            P("groups", None, "lat", ("lon", "cl")),
            P("groups", None, "lat", ("lon", "cl")),
            P("groups", None, "lat", ("lon", "cl")),
            P(("groups", "lon", "lat"), None, None),
            P(("groups", "lon", "lat"), None, None, None),
            P(("groups", "lon", "lat"), None, None),
        ),
        check_vma=False,
    )
```

```python
import functools

import jax
import jax.numpy as jnp
from jax import lax
from jax.experimental import pallas as pl
from jax.experimental.pallas import tpu as pltpu
from jax.sharding import PartitionSpec as P

STEPS = 2


def padded_2(value, sides, width, wrap):
    for axis, dim in sides:
        size, length = (lax.axis_size(axis), value.shape[dim])
        up = [(i, (i + 1) % size) for i in range(size if wrap else size - 1)]
        down = [(j, i) for i, j in up]
        last = lax.slice_in_dim(value, length - width, length, axis=dim)
        leading = lax.slice_in_dim(value, 0, width, axis=dim)
        before = lax.ppermute(last, axis, up)
        after = lax.ppermute(leading, axis, down)
        value = jnp.concatenate([before, value, after], axis=dim)
    return value


def build_table(diffusivity, east_peclet, north_peclet, sea_mask, depth_levels):
    levels = lax.broadcasted_iota(jnp.int32, diffusivity.shape, 0)
    active = (levels < depth_levels[None]).astype(jnp.float32) * sea_mask[None].astype(jnp.float32)
    return jnp.stack(
        [
            diffusivity * (1.0 - east_peclet),
            diffusivity * (1.0 + east_peclet),
            diffusivity * (1.0 - north_peclet),
            diffusivity * (1.0 + north_peclet),
            4.0 * diffusivity,
            active,
        ]
    )


def with_rims(grid_values, width):
    padded = padded_2(grid_values, (("lat", 2),), width, False)
    return padded_2(padded, ((("lon", "cl"), 3),), width, True)


def advance(padded, coefficients):
    inner_coef = coefficients[:, :, 1:-1, 1:-1]
    interior = padded[:, :, 1:-1, 1:-1]
    change = inner_coef[0] * padded[:, :, 1:-1, 2:] + inner_coef[1] * padded[:, :, 1:-1, :-2]
    change = (
        change + inner_coef[2] * padded[:, :, 2:, 1:-1] + inner_coef[3] * padded[:, :, :-2, 1:-1]
    )
    return interior + inner_coef[5] * (change - inner_coef[4] * interior)


def retreat(padded, coefficients):
    pushed = coefficients[5] * padded
    summed = padded[:, :, 1:-1, 1:-1] - (coefficients[4] * pushed)[:, :, 1:-1, 1:-1]
    summed = (
        summed
        + (coefficients[0] * pushed)[:, :, 1:-1, :-2]
        + (coefficients[1] * pushed)[:, :, 1:-1, 2:]
    )
    summed = (
        summed
        + (coefficients[2] * pushed)[:, :, :-2, 1:-1]
        + (coefficients[3] * pushed)[:, :, 2:, 1:-1]
    )
    return summed


def sweep_steps(grid_values, coefficients, update):
    for number in range(STEPS):
        grid_values = update(with_rims(grid_values, 1), coefficients)
    return grid_values


def project(left, right):
    return jnp.dot(left, right, preferred_element_type=jnp.float32)


def project_back(left, right):
    return lax.dot_general(
        left, right, (((1,), (1,)), ((), ())), preferred_element_type=jnp.float32
    )


def contract_rows(left, right):
    return lax.dot_general(
        left, right, (((0,), (0,)), ((), ())), preferred_element_type=jnp.float32
    )


def closure_pass(inputs, pushed, w_in, w_mid, w_out):
    slopes = []
    layers = [inputs]
    shaped = jnp.tanh(project(inputs, w_in))
    slopes.append(1.0 - shaped * shaped)
    acting = shaped.astype(jnp.bfloat16)
    layers.append(acting)
    layer_index = 0
    shaped = jnp.tanh(project(acting, w_mid[layer_index]))
    slopes.append(1.0 - shaped * shaped)
    acting = shaped.astype(jnp.bfloat16)
    layers.append(acting)
    raw_tend = project(acting, w_out).astype(jnp.bfloat16)
    grad_out = contract_rows(acting, pushed)
    backward = project_back(pushed, w_out)
    mid_grads = []
    for layer_index in reversed(range(w_mid.shape[0])):
        deltas = (backward * slopes[layer_index + 1]).astype(jnp.bfloat16)
        mid_grads.append(contract_rows(layers[layer_index + 1], deltas))
        backward = project_back(deltas, w_mid[layer_index])
    deltas = (backward * slopes[0]).astype(jnp.bfloat16)
    grad_in = contract_rows(inputs, deltas)
    back_in = project_back(deltas, w_in).astype(jnp.bfloat16)
    return (raw_tend, back_in, grad_in, jnp.stack(mid_grads[::-1]), grad_out)


def on_device(
    ocean_state,
    cotangent,
    diffusivity,
    east_peclet,
    north_peclet,
    sea_mask,
    depth_levels,
    owner_table,
    w_in,
    w_mid,
    w_out,
):
    coefficients = build_table(diffusivity, east_peclet, north_peclet, sea_mask, depth_levels)
    active = coefficients[5]
    rim_width = 1
    coef_rims = with_rims(coefficients, rim_width)
    advected = sweep_steps(ocean_state, coef_rims, advance)
    features = ocean_state.shape[0] * ocean_state.shape[1]
    columns = ocean_state.shape[2] * ocean_state.shape[3]
    experts = lax.axis_size(("lon", "lat"))
    capacity = 2 * columns // experts
    owners = owner_table.reshape(columns)
    one_hot = (owners[:, None] == lax.broadcasted_iota(jnp.int32, (columns, experts), 1)).astype(
        jnp.int32
    )
    rank_in = jnp.sum(jnp.cumsum(one_hot, axis=0) * one_hot, axis=1) - 1
    slot_index = owners * capacity + rank_in
    col_inputs = advected.reshape(features, columns).T.astype(jnp.bfloat16)
    col_pushed = (active[None] * cotangent).reshape(features, columns).T.astype(jnp.bfloat16)
    empty = jnp.zeros((experts * capacity, features), jnp.bfloat16)
    send_inputs = empty.at[slot_index].set(col_inputs)
    send_pushed = empty.at[slot_index].set(col_pushed)
    got_inputs, got_pushed = (
        lax.all_to_all(send_inputs, ("lon", "lat"), split_axis=0, concat_axis=0, tiled=True),
        lax.all_to_all(send_pushed, ("lon", "lat"), split_axis=0, concat_axis=0, tiled=True),
    )
    raw_tend, back_in, grad_in, grad_mid, grad_out = closure_pass(
        got_inputs, got_pushed, w_in[0], w_mid[0], w_out[0]
    )
    grad_in, grad_mid, grad_out = lax.psum((grad_in, grad_mid, grad_out), "cl")
    ret_tend, ret_back = (
        lax.all_to_all(raw_tend, ("lon", "lat"), split_axis=0, concat_axis=0, tiled=True),
        lax.all_to_all(back_in, ("lon", "lat"), split_axis=0, concat_axis=0, tiled=True),
    )
    tend_grid = ret_tend[slot_index].T.reshape(ocean_state.shape)
    back_grid = ret_back[slot_index].T.reshape(ocean_state.shape)
    tendency = (active[None] * tend_grid.astype(jnp.float32)).astype(jnp.bfloat16)
    adjoint_start = cotangent + back_grid.astype(jnp.float32)
    state_grad = sweep_steps(adjoint_start, coef_rims, retreat)
    return (advected, tendency, state_grad, grad_in[None], grad_mid[None], grad_out[None])


MESH = pl.DeviceIdType.MESH
VMEM_BYTES = 61 * 1024 * 1024


def matmul(left, right, contract):
    return lax.dot_general(
        left, right, (((contract[0],), (contract[1],)), ((), ())),
        preferred_element_type=jnp.float32,
    )


def tile_kernel(
    n_lon, n_lat, n_cl, cap,
    x_hbm, cot_hbm, diff_hbm, ep_hbm, np_hbm, sea_hbm, dep_hbm, own_hbm, wi_hbm, wm_hbm, wo_hbm,
    adv_hbm, tend_hbm, sg_hbm, gi_hbm, gm_hbm, go_hbm,
    x_ref, cot_ref, diff_ref, ep_ref, np_ref, sea_ref, dep_ref, own_ref, wi_ref, wm_ref, wo_ref,
    adv_ref, tend_ref, sg_ref, gi_ref, gm_ref, go_ref, load_sem, store_sem, d8, tmp, hal, lat_s, lat_r, lon_s, lon_r, pt, snd, rcv, gis, gms, gos, gir, gmr, gor,
    lat_ss, lat_rs, lon_ss, lon_rs, a2a_ss, a2a_rs, g_ss, g_rs,
):
    experts = n_lon * n_lat
    lon, lat, cl = lax.axis_index("lon"), lax.axis_index("lat"), lax.axis_index("cl")
    ring = n_lon * n_cl
    place = lon * n_cl + cl
    east, west = (place + 1) % ring, (place + ring - 1) % ring
    east_id = {"lon": east // n_cl, "cl": east % n_cl}
    west_id = {"lon": west // n_cl, "cl": west % n_cl}
    lat_id = {"lat": 1 - lat}
    cl_id = {"cl": 1 - cl}
    me = lon * n_lat + lat
    partners = [(me + d) % experts for d in range(experts)]
    partner_ids = [{"lon": p // n_lat, "lat": p % n_lat} for p in partners]

    barrier = pltpu.get_barrier_semaphore()
    for other in partner_ids[1:] + [east_id, west_id]:
        pl.semaphore_signal(barrier, inc=1, device_id=other, device_id_type=MESH)

    loads = {}
    for i, (name, src, dst) in enumerate((
        ("x", x_hbm, x_ref), ("diff", diff_hbm, diff_ref), ("ep", ep_hbm, ep_ref),
        ("np", np_hbm, np_ref), ("sea", sea_hbm, sea_ref), ("dep", dep_hbm, dep_ref),
        ("own", own_hbm, own_ref), ("cot", cot_hbm, cot_ref), ("wo", wo_hbm, wo_ref),
        ("wi", wi_hbm, wi_ref), ("wm", wm_hbm, wm_ref),
    )):
        loads[name] = pltpu.make_async_copy(src, dst, load_sem.at[i])
        loads[name].start()

    results = (
        (adv_ref, adv_hbm), (tend_ref, tend_hbm), (sg_ref, sg_hbm),
        (gi_ref, gi_hbm), (gm_ref, gm_hbm), (go_ref, go_hbm),
    )
    stores = [
        pltpu.make_async_copy(a, b, store_sem.at[i]) for i, (a, b) in enumerate(results)
    ]

    rows, wide = x_ref.shape
    tiles = rows // 8
    fields = rows // diff_ref.shape[0]
    feats = rows // 4
    cube = (tiles, 8, wide)
    four = (fields, tiles // fields, 8, wide)
    lane = lax.broadcasted_iota(jnp.int32, cube, 2)
    tile = lax.broadcasted_iota(jnp.int32, cube, 0)
    row = lax.broadcasted_iota(jnp.int32, cube, 1) % 4
    on_tile = lane == tile
    south = jnp.full(cube, lat, jnp.int32) == 0

    for name in ("sea", "dep", "diff", "ep", "np"):
        loads[name].wait()
    d8[0, 0:4], d8[0, 4:8] = sea_ref[...], sea_ref[...]
    d8[1, 0:4], d8[1, 4:8] = dep_ref[...], dep_ref[...]
    flat = (tiles // fields, 8, wide)
    level = 2 * lax.broadcasted_iota(jnp.int32, flat, 0) + (
        lax.broadcasted_iota(jnp.int32, flat, 1) // 4
    )
    diff = diff_ref[...].reshape(flat)
    ep, np_ = ep_ref[...].reshape(flat), np_ref[...].reshape(flat)
    active = (level < d8[1][None]).astype(jnp.float32) * d8[0][None].astype(jnp.float32)
    c_e, c_w = (diff * (1.0 - ep))[None], (diff * (1.0 + ep))[None]
    c_n, c_s = (diff * (1.0 - np_))[None], (diff * (1.0 + np_))[None]
    c_0, act = (4.0 * diff)[None], active[None]

    def pack(value, side):
        return jnp.sum(jnp.where(on_tile, value[:, :, side : side + 1], 0.0), axis=0)

    def unpack(packed):
        return jnp.sum(jnp.where(on_tile, packed[None], 0.0), axis=2, keepdims=True)

    def send_edges(number, to_e, to_w, to_n, to_s):
        tmp[...] = jnp.where(south, to_n, to_s).reshape(rows, wide)
        pick = jnp.full((feats, wide), lat, jnp.int32) == 0
        lat_s[number] = jnp.where(
            pick, tmp[pl.ds(3, feats, stride=4), :], tmp[pl.ds(0, feats, stride=4), :]
        ).astype(jnp.bfloat16)
        lon_s[number, 0] = pack(to_e, wide - 1)
        lon_s[number, 1] = pack(to_w, 0)
        copies = [
            pltpu.make_async_remote_copy(
                lat_s.at[number], lat_r.at[number], lat_ss.at[number], lat_rs.at[number],
                device_id=lat_id, device_id_type=MESH,
            ),
            pltpu.make_async_remote_copy(
                lon_s.at[number, 0], lon_r.at[number, 0],
                lon_ss.at[number, 0], lon_rs.at[number, 0],
                device_id=east_id, device_id_type=MESH,
            ),
            pltpu.make_async_remote_copy(
                lon_s.at[number, 1], lon_r.at[number, 1],
                lon_ss.at[number, 1], lon_rs.at[number, 1],
                device_id=west_id, device_id_type=MESH,
            ),
        ]
        for copy in copies:
            copy.start()
        return copies

    def shifted(number, copies, to_e, to_w, to_n, to_s):
        for copy in copies:
            copy.wait()
        from_w = jnp.where(lane == 0, unpack(lon_r[number, 0]), pltpu.roll(to_e, 1, 2))
        from_e = jnp.where(
            lane == wide - 1, unpack(lon_r[number, 1]), pltpu.roll(to_w, wide - 1, 2)
        )
        beyond = lat_r[number].astype(jnp.float32)
        hal[pl.ds(0, feats, stride=4), :] = beyond
        hal[pl.ds(3, feats, stride=4), :] = beyond
        edge = hal[...].reshape(cube)
        from_s = jnp.where(row == 0, jnp.where(south, 0.0, edge), pltpu.roll(to_n, 1, 1))
        from_n = jnp.where(row == 3, jnp.where(south, edge, 0.0), pltpu.roll(to_s, 7, 1))
        return [v.reshape(four) for v in (from_w, from_e, from_s, from_n)]

    def exchange(kind):
        copies = []
        for d in range(1, experts):
            copies.append(
                pltpu.make_async_remote_copy(
                    snd.at[kind, partners[d]], rcv.at[kind, me],
                    a2a_ss.at[kind, d], a2a_rs.at[kind, d],
                    device_id=partner_ids[d], device_id_type=MESH,
                )
            )
            copies[-1].start()
        rcv[kind, me] = snd[kind, me]
        return copies

    def arrived(kind, copies):
        for copy in copies:
            copy.wait()
        return jnp.concatenate([rcv[kind, e] for e in range(experts)], axis=1)

    def columns_of(ref):
        return jnp.concatenate(
            [ref[pl.ds(i, feats, stride=4), :] for i in range(4)], axis=1
        ).astype(jnp.bfloat16)

    def to_slots(kind, columns):
        slots = matmul(columns, pt[...], (1, 1)).astype(jnp.bfloat16)
        for e in range(experts):
            snd[kind, e] = slots[:, e * cap : (e + 1) * cap]

    def to_grid(slots):
        columns = matmul(slots, pt[...], (1, 0))
        for i in range(4):
            tmp[pl.ds(i, feats, stride=4), :] = columns[:, i * wide : (i + 1) * wide]
        return tmp[...].reshape(four)

    loads["x"].wait()
    state = x_ref[...].reshape(four)
    whole = state.reshape(cube)
    pl.semaphore_wait(barrier, experts - 1 + 2)
    copies = send_edges(0, whole, whole, whole, whole)

    for name in ("own", "cot"):
        loads[name].wait()
    count = 4 * wide
    owners = jnp.concatenate([own_ref[i : i + 1, :] for i in range(4)], axis=1)
    hot = (owners == lax.broadcasted_iota(jnp.int32, (experts, count), 0)).astype(jnp.float32)
    before = (
        lax.broadcasted_iota(jnp.int32, (count, count), 0)
        < lax.broadcasted_iota(jnp.int32, (count, count), 1)
    ).astype(jnp.float32).astype(jnp.bfloat16)
    earlier = matmul(hot.astype(jnp.bfloat16), before, (1, 0))
    rank = jnp.sum(hot * earlier, axis=0, keepdims=True)
    slot = owners * cap + rank.astype(jnp.int32)
    pt[...] = (
        lax.broadcasted_iota(jnp.int32, (experts * cap, count), 0) == slot
    ).astype(jnp.float32).astype(jnp.bfloat16)

    cot = cot_ref[...].reshape(four)
    tmp[...] = (act * cot).reshape(rows, wide)
    to_slots(0, columns_of(tmp))
    sent = exchange(0)

    for number in range(STEPS):
        if number > 0:
            whole = state.reshape(cube)
            copies = send_edges(number, whole, whole, whole, whole)
        from_w, from_e, from_s, from_n = shifted(number, copies, whole, whole, whole, whole)
        change = c_e * from_e + c_w * from_w + c_n * from_n + c_s * from_s
        state = state + act * (change - c_0 * state)
    adv_ref[...] = state.reshape(rows, wide)
    to_slots(1, columns_of(adv_ref))
    sent_in = exchange(1)
    stores[0].start()
    for name in ("wo", "wi", "wm"):
        loads[name].wait()
    pushed = arrived(0, sent)
    back_2 = matmul(wo_ref[...], pushed, (1, 0))
    inputs = arrived(1, sent_in)

    t_0 = jnp.tanh(matmul(wi_ref[...], inputs, (0, 0)))
    a_0 = t_0.astype(jnp.bfloat16)
    t_1 = jnp.tanh(matmul(wm_ref[...], a_0, (0, 0)))
    a_1 = t_1.astype(jnp.bfloat16)
    delta_1 = (back_2 * (1.0 - t_1 * t_1)).astype(jnp.bfloat16)
    back_1 = matmul(wm_ref[...], delta_1, (1, 0))
    delta_0 = (back_1 * (1.0 - t_0 * t_0)).astype(jnp.bfloat16)
    back_in = matmul(wi_ref[...], delta_0, (1, 0)).astype(jnp.bfloat16)
    for e in range(experts):
        snd[2, e] = back_in[:, e * cap : (e + 1) * cap]
    sent_back = exchange(2)
    raw = matmul(wo_ref[...], a_1, (0, 0)).astype(jnp.bfloat16)
    for e in range(experts):
        snd[3, e] = raw[:, e * cap : (e + 1) * cap]
    gis[...] = matmul(inputs, delta_0, (1, 1))
    gms[...] = matmul(a_0, delta_1, (1, 1))
    gos[...] = matmul(a_1, pushed, (1, 1))
    sent_grads = []
    for i, (src, dst) in enumerate(((gis, gir), (gms, gmr), (gos, gor))):
        sent_grads.append(
            pltpu.make_async_remote_copy(
                src, dst, g_ss.at[i], g_rs.at[i], device_id=cl_id, device_id_type=MESH
            )
        )
        sent_grads[-1].start()

    grad = cot + to_grid(arrived(2, sent_back))
    for number in range(STEPS, 2 * STEPS):
        held = act * grad
        parts = [(c * held).reshape(cube) for c in (c_e, c_w, c_n, c_s)]
        copies = send_edges(number, *parts)
        if number == STEPS:
            sent_raw = exchange(3)
        base = grad - c_0 * held
        if number == 2 * STEPS - 1:
            tend = arrived(3, sent_raw)
        from_w, from_e, from_s, from_n = shifted(number, copies, *parts)
        grad = base + from_w + from_e + from_s + from_n
    sg_ref[...] = grad.reshape(rows, wide)
    stores[2].start()
    tend_ref[...] = (act * to_grid(tend)).reshape(rows, wide).astype(jnp.bfloat16)
    stores[1].start()
    for copy in sent_grads:
        copy.wait()
    gi_ref[...] = gis[...] + gir[...]
    gm_ref[...] = gms[...] + gmr[...]
    go_ref[...] = gos[...] + gor[...]
    for copy in stores[3:]:
        copy.start()
    for copy in stores:
        copy.wait()


def store_kernel(*refs):
    sems = refs[-1]
    loads = [pltpu.make_async_copy(refs[i], refs[i + 12], sems.at[0, i]) for i in range(6)]
    stores = [pltpu.make_async_copy(refs[i + 12], refs[i + 6], sems.at[1, i]) for i in range(6)]
    for copy in loads:
        copy.start()
    for load, store in zip(loads, stores):
        load.wait()
        store.start()
    for copy in stores:
        copy.wait()


def on_device_fused(
    ocean_state, cotangent, diffusivity, east_peclet, north_peclet, sea_mask, depth_levels,
    owner_table, w_in, w_mid, w_out,
):
    n_lon, n_lat, n_cl = (lax.axis_size(axis) for axis in ("lon", "lat", "cl"))
    wide = ocean_state.shape[3]
    rows = ocean_state.size // wide
    columns = 4 * wide
    experts = n_lon * n_lat
    cap = 2 * columns // experts
    feats, hidden = w_in.shape[1:]
    f32, bf16 = jnp.float32, jnp.bfloat16
    sizes = [(rows, wide)] * 3 + [(feats, hidden), (hidden, hidden), (hidden, feats)]
    results = [
        jax.ShapeDtypeStruct(size, bf16 if i == 1 else f32) for i, size in enumerate(sizes)
    ]
    flat = lambda v: v.reshape(-1, wide)
    hbm = pl.BlockSpec(memory_space=pltpu.HBM)
    operands = (
        flat(ocean_state), flat(cotangent), flat(diffusivity), flat(east_peclet),
        flat(north_peclet), sea_mask, depth_levels, flat(owner_table), w_in[0], w_mid[0, 0],
        w_out[0],
    )
    out = pl.pallas_call(
        functools.partial(tile_kernel, n_lon, n_lat, n_cl, cap),
        out_shape=results,
        in_specs=[hbm] * 11,
        out_specs=[hbm] * 6,
        scratch_shapes=[pltpu.VMEM(v.shape, v.dtype) for v in (*operands, *results)]
        + [
            pltpu.SemaphoreType.DMA((11,)),
            pltpu.SemaphoreType.DMA((6,)),
            pltpu.VMEM((2, 8, wide), jnp.int32),
            pltpu.VMEM((rows, wide), f32),
            pltpu.VMEM((rows, wide), f32),
            pltpu.VMEM((2 * STEPS, feats, wide), bf16),
            pltpu.VMEM((2 * STEPS, feats, wide), bf16),
            pltpu.VMEM((2 * STEPS, 2, 8, wide), f32),
            pltpu.VMEM((2 * STEPS, 2, 8, wide), f32),
            pltpu.VMEM((experts * cap, columns), bf16),
            pltpu.VMEM((4, experts, feats, cap), bf16),
            pltpu.VMEM((4, experts, feats, cap), bf16),
        ]
        + [pltpu.VMEM(s, f32) for s in ((feats, hidden), (hidden, hidden), (hidden, feats))] * 2
        + [pltpu.SemaphoreType.DMA((2 * STEPS,))] * 2
        + [pltpu.SemaphoreType.DMA((2 * STEPS, 2))] * 2
        + [pltpu.SemaphoreType.DMA((4, experts))] * 2
        + [pltpu.SemaphoreType.DMA((3,))] * 2,
        compiler_params=pltpu.CompilerParams(
            collective_id=0, has_side_effects=True, vmem_limit_bytes=VMEM_BYTES
        ),
    )(*operands)
    out = pl.pallas_call(
        store_kernel,
        out_shape=results,
        in_specs=[hbm] * 6,
        out_specs=[hbm] * 6,
        scratch_shapes=[pltpu.VMEM(v.shape, v.dtype) for v in results]
        + [pltpu.SemaphoreType.DMA((2, 6))],
        compiler_params=pltpu.CompilerParams(vmem_limit_bytes=VMEM_BYTES),
    )(*out)
    advected, tendency, state_grad, grad_in, grad_mid, grad_out = out
    shape = ocean_state.shape
    return (
        advected.reshape(shape), tendency.reshape(shape), state_grad.reshape(shape),
        grad_in[None], grad_mid[None, None], grad_out[None],
    )


def solution(mesh):
    few = mesh.shape["lat"] == 2 and mesh.shape["cl"] == 2 and 2 < mesh.shape["lon"] <= 4
    plan = on_device_fused if few else on_device
    return jax.shard_map(
        plan,
        mesh=mesh,
        in_specs=(
            P("groups", None, "lat", ("lon", "cl")),
            P("groups", None, "lat", ("lon", "cl")),
            P(None, "lat", ("lon", "cl")),
            P(None, "lat", ("lon", "cl")),
            P(None, "lat", ("lon", "cl")),
            P("lat", ("lon", "cl")),
            P("lat", ("lon", "cl")),
            P("lat", ("lon", "cl"), None, None),
            P(("lon", "lat"), None, None),
            P(("lon", "lat"), None, None, None),
            P(("lon", "lat"), None, None),
        ),
        out_specs=(
            P("groups", None, "lat", ("lon", "cl")),
            P("groups", None, "lat", ("lon", "cl")),
            P("groups", None, "lat", ("lon", "cl")),
            P(("groups", "lon", "lat"), None, None),
            P(("groups", "lon", "lat"), None, None, None),
            P(("groups", "lon", "lat"), None, None),
        ),
        check_vma=False,
    )
```

```python
import functools

import jax
import jax.numpy as jnp
from jax import lax
from jax.experimental import pallas as pl
from jax.experimental.pallas import tpu as pltpu
from jax.sharding import PartitionSpec as P

STEPS = 2


def padded_2(value, sides, width, wrap):
    for axis, dim in sides:
        size, length = (lax.axis_size(axis), value.shape[dim])
        up = [(i, (i + 1) % size) for i in range(size if wrap else size - 1)]
        down = [(j, i) for i, j in up]
        last = lax.slice_in_dim(value, length - width, length, axis=dim)
        leading = lax.slice_in_dim(value, 0, width, axis=dim)
        before = lax.ppermute(last, axis, up)
        after = lax.ppermute(leading, axis, down)
        value = jnp.concatenate([before, value, after], axis=dim)
    return value


def build_table(diffusivity, east_peclet, north_peclet, sea_mask, depth_levels):
    levels = lax.broadcasted_iota(jnp.int32, diffusivity.shape, 0)
    active = (levels < depth_levels[None]).astype(jnp.float32) * sea_mask[None].astype(jnp.float32)
    return jnp.stack(
        [
            diffusivity * (1.0 - east_peclet),
            diffusivity * (1.0 + east_peclet),
            diffusivity * (1.0 - north_peclet),
            diffusivity * (1.0 + north_peclet),
            4.0 * diffusivity,
            active,
        ]
    )


def with_rims(grid_values, width):
    padded = padded_2(grid_values, (("lat", 2),), width, False)
    return padded_2(padded, ((("lon", "cl"), 3),), width, True)


def advance(padded, coefficients):
    inner_coef = coefficients[:, :, 1:-1, 1:-1]
    interior = padded[:, :, 1:-1, 1:-1]
    change = inner_coef[0] * padded[:, :, 1:-1, 2:] + inner_coef[1] * padded[:, :, 1:-1, :-2]
    change = (
        change + inner_coef[2] * padded[:, :, 2:, 1:-1] + inner_coef[3] * padded[:, :, :-2, 1:-1]
    )
    return interior + inner_coef[5] * (change - inner_coef[4] * interior)


def retreat(padded, coefficients):
    pushed = coefficients[5] * padded
    summed = padded[:, :, 1:-1, 1:-1] - (coefficients[4] * pushed)[:, :, 1:-1, 1:-1]
    summed = (
        summed
        + (coefficients[0] * pushed)[:, :, 1:-1, :-2]
        + (coefficients[1] * pushed)[:, :, 1:-1, 2:]
    )
    summed = (
        summed
        + (coefficients[2] * pushed)[:, :, :-2, 1:-1]
        + (coefficients[3] * pushed)[:, :, 2:, 1:-1]
    )
    return summed


def sweep_steps(grid_values, coefficients, update):
    for number in range(STEPS):
        grid_values = update(with_rims(grid_values, 1), coefficients)
    return grid_values


def project(left, right):
    return jnp.dot(left, right, preferred_element_type=jnp.float32)


def project_back(left, right):
    return lax.dot_general(
        left, right, (((1,), (1,)), ((), ())), preferred_element_type=jnp.float32
    )


def contract_rows(left, right):
    return lax.dot_general(
        left, right, (((0,), (0,)), ((), ())), preferred_element_type=jnp.float32
    )


def closure_pass(inputs, pushed, w_in, w_mid, w_out):
    slopes = []
    layers = [inputs]
    shaped = jnp.tanh(project(inputs, w_in))
    slopes.append(1.0 - shaped * shaped)
    acting = shaped.astype(jnp.bfloat16)
    layers.append(acting)
    layer_index = 0
    shaped = jnp.tanh(project(acting, w_mid[layer_index]))
    slopes.append(1.0 - shaped * shaped)
    acting = shaped.astype(jnp.bfloat16)
    layers.append(acting)
    raw_tend = project(acting, w_out).astype(jnp.bfloat16)
    grad_out = contract_rows(acting, pushed)
    backward = project_back(pushed, w_out)
    mid_grads = []
    for layer_index in reversed(range(w_mid.shape[0])):
        deltas = (backward * slopes[layer_index + 1]).astype(jnp.bfloat16)
        mid_grads.append(contract_rows(layers[layer_index + 1], deltas))
        backward = project_back(deltas, w_mid[layer_index])
    deltas = (backward * slopes[0]).astype(jnp.bfloat16)
    grad_in = contract_rows(inputs, deltas)
    back_in = project_back(deltas, w_in).astype(jnp.bfloat16)
    return (raw_tend, back_in, grad_in, jnp.stack(mid_grads[::-1]), grad_out)


def on_device(
    ocean_state,
    cotangent,
    diffusivity,
    east_peclet,
    north_peclet,
    sea_mask,
    depth_levels,
    owner_table,
    w_in,
    w_mid,
    w_out,
):
    coefficients = build_table(diffusivity, east_peclet, north_peclet, sea_mask, depth_levels)
    active = coefficients[5]
    rim_width = 1
    coef_rims = with_rims(coefficients, rim_width)
    advected = sweep_steps(ocean_state, coef_rims, advance)
    features = ocean_state.shape[0] * ocean_state.shape[1]
    columns = ocean_state.shape[2] * ocean_state.shape[3]
    experts = lax.axis_size(("lon", "lat"))
    capacity = 2 * columns // experts
    owners = owner_table.reshape(columns)
    one_hot = (owners[:, None] == lax.broadcasted_iota(jnp.int32, (columns, experts), 1)).astype(
        jnp.int32
    )
    rank_in = jnp.sum(jnp.cumsum(one_hot, axis=0) * one_hot, axis=1) - 1
    slot_index = owners * capacity + rank_in
    col_inputs = advected.reshape(features, columns).T.astype(jnp.bfloat16)
    col_pushed = (active[None] * cotangent).reshape(features, columns).T.astype(jnp.bfloat16)
    empty = jnp.zeros((experts * capacity, features), jnp.bfloat16)
    send_inputs = empty.at[slot_index].set(col_inputs)
    send_pushed = empty.at[slot_index].set(col_pushed)
    got_inputs, got_pushed = (
        lax.all_to_all(send_inputs, ("lon", "lat"), split_axis=0, concat_axis=0, tiled=True),
        lax.all_to_all(send_pushed, ("lon", "lat"), split_axis=0, concat_axis=0, tiled=True),
    )
    raw_tend, back_in, grad_in, grad_mid, grad_out = closure_pass(
        got_inputs, got_pushed, w_in[0], w_mid[0], w_out[0]
    )
    grad_in, grad_mid, grad_out = lax.psum((grad_in, grad_mid, grad_out), "cl")
    ret_tend, ret_back = (
        lax.all_to_all(raw_tend, ("lon", "lat"), split_axis=0, concat_axis=0, tiled=True),
        lax.all_to_all(back_in, ("lon", "lat"), split_axis=0, concat_axis=0, tiled=True),
    )
    tend_grid = ret_tend[slot_index].T.reshape(ocean_state.shape)
    back_grid = ret_back[slot_index].T.reshape(ocean_state.shape)
    tendency = (active[None] * tend_grid.astype(jnp.float32)).astype(jnp.bfloat16)
    adjoint_start = cotangent + back_grid.astype(jnp.float32)
    state_grad = sweep_steps(adjoint_start, coef_rims, retreat)
    return (advected, tendency, state_grad, grad_in[None], grad_mid[None], grad_out[None])


MESH = pl.DeviceIdType.MESH
VMEM_BYTES = 61 * 1024 * 1024


def matmul(left, right, contract):
    return lax.dot_general(
        left, right, (((contract[0],), (contract[1],)), ((), ())),
        preferred_element_type=jnp.float32,
    )


def tile_kernel(
    n_lon, n_lat, n_cl, cap,
    x_hbm, cot_hbm, diff_hbm, ep_hbm, np_hbm, sea_hbm, dep_hbm, own_hbm, wi_hbm, wm_hbm, wo_hbm,
    adv_hbm, tend_hbm, sg_hbm, gi_hbm, gm_hbm, go_hbm,
    x_ref, cot_ref, diff_ref, ep_ref, np_ref, sea_ref, dep_ref, own_ref, wi_ref, wm_ref, wo_ref,
    adv_ref, tend_ref, sg_ref, gi_ref, gm_ref, go_ref, load_sem, store_sem, d8, tmp, hal, lat_s, lat_r, lon_s, lon_r, pt, snd, rcv,
    wi_far, wm_far, wo_far, gi_own, gm_own, go_own, gi_far, gm_far, go_far,
    gi_one, gm_one, go_one, gi_two, gm_two, go_two,
    gi_out, gm_out, go_out, gi_got, gm_got, go_got,
    lat_ss, lat_rs, lon_ss, lon_rs, a2a_ss, a2a_rs, w_ss, w_rs, g_ss, g_rs,
):
    experts = n_lon * n_lat
    lon, lat, cl = lax.axis_index("lon"), lax.axis_index("lat"), lax.axis_index("cl")
    ring = n_lon * n_cl
    place = lon * n_cl + cl
    east, west = (place + 1) % ring, (place + ring - 1) % ring
    east_id = {"lon": east // n_cl, "cl": east % n_cl}
    west_id = {"lon": west // n_cl, "cl": west % n_cl}
    lat_id = {"lat": 1 - lat}
    cl_id = {"cl": 1 - cl}
    deep = n_lon // 2
    members = deep * n_lat
    half = lon // deep
    me = (lon % deep) * n_lat + lat
    partners = [(me + d) % members for d in range(members)]
    partner_ids = [{"lon": half * deep + p // n_lat, "lat": p % n_lat} for p in partners]
    far_id = {"lon": (lon + deep) % n_lon}

    barrier = pltpu.get_barrier_semaphore()
    for other in partner_ids[1:] + [east_id, west_id, far_id]:
        pl.semaphore_signal(barrier, inc=1, device_id=other, device_id_type=MESH)

    loads = {}
    for i, (name, src, dst) in enumerate((
        ("x", x_hbm, x_ref), ("diff", diff_hbm, diff_ref), ("ep", ep_hbm, ep_ref),
        ("np", np_hbm, np_ref), ("sea", sea_hbm, sea_ref), ("dep", dep_hbm, dep_ref),
        ("own", own_hbm, own_ref), ("cot", cot_hbm, cot_ref), ("wo", wo_hbm, wo_ref),
        ("wi", wi_hbm, wi_ref), ("wm", wm_hbm, wm_ref),
    )):
        loads[name] = pltpu.make_async_copy(src, dst, load_sem.at[i])
        loads[name].start()

    results = (
        (adv_ref, adv_hbm), (tend_ref, tend_hbm), (sg_ref, sg_hbm),
        (gi_ref, gi_hbm), (gm_ref, gm_hbm), (go_ref, go_hbm),
    )
    stores = [
        pltpu.make_async_copy(a, b, store_sem.at[i]) for i, (a, b) in enumerate(results)
    ]

    rows, wide = x_ref.shape
    tiles = rows // 8
    fields = rows // diff_ref.shape[0]
    feats = rows // 4
    cube = (tiles, 8, wide)
    four = (fields, tiles // fields, 8, wide)
    lane = lax.broadcasted_iota(jnp.int32, cube, 2)
    tile = lax.broadcasted_iota(jnp.int32, cube, 0)
    row = lax.broadcasted_iota(jnp.int32, cube, 1) % 4
    on_tile = lane == tile
    south = jnp.full(cube, lat, jnp.int32) == 0

    for name in ("sea", "dep", "diff", "ep", "np"):
        loads[name].wait()
    d8[0, 0:4], d8[0, 4:8] = sea_ref[...], sea_ref[...]
    d8[1, 0:4], d8[1, 4:8] = dep_ref[...], dep_ref[...]
    flat = (tiles // fields, 8, wide)
    level = 2 * lax.broadcasted_iota(jnp.int32, flat, 0) + (
        lax.broadcasted_iota(jnp.int32, flat, 1) // 4
    )
    diff = diff_ref[...].reshape(flat)
    ep, np_ = ep_ref[...].reshape(flat), np_ref[...].reshape(flat)
    active = (level < d8[1][None]).astype(jnp.float32) * d8[0][None].astype(jnp.float32)
    c_e, c_w = (diff * (1.0 - ep))[None], (diff * (1.0 + ep))[None]
    c_n, c_s = (diff * (1.0 - np_))[None], (diff * (1.0 + np_))[None]
    c_0, act = (4.0 * diff)[None], active[None]

    def pack(value, side):
        return jnp.sum(jnp.where(on_tile, value[:, :, side : side + 1], 0.0), axis=0)

    def unpack(packed):
        return jnp.sum(jnp.where(on_tile, packed[None], 0.0), axis=2, keepdims=True)

    def send_edges(number, to_e, to_w, to_n, to_s):
        tmp[...] = jnp.where(south, to_n, to_s).reshape(rows, wide)
        pick = jnp.full((feats, wide), lat, jnp.int32) == 0
        lat_s[number] = jnp.where(
            pick, tmp[pl.ds(3, feats, stride=4), :], tmp[pl.ds(0, feats, stride=4), :]
        ).astype(jnp.bfloat16)
        lon_s[number, 0] = pack(to_e, wide - 1)
        lon_s[number, 1] = pack(to_w, 0)
        copies = [
            pltpu.make_async_remote_copy(
                lat_s.at[number], lat_r.at[number], lat_ss.at[number], lat_rs.at[number],
                device_id=lat_id, device_id_type=MESH,
            ),
            pltpu.make_async_remote_copy(
                lon_s.at[number, 0], lon_r.at[number, 0],
                lon_ss.at[number, 0], lon_rs.at[number, 0],
                device_id=east_id, device_id_type=MESH,
            ),
            pltpu.make_async_remote_copy(
                lon_s.at[number, 1], lon_r.at[number, 1],
                lon_ss.at[number, 1], lon_rs.at[number, 1],
                device_id=west_id, device_id_type=MESH,
            ),
        ]
        for copy in copies:
            copy.start()
        return copies

    def shifted(number, copies, to_e, to_w, to_n, to_s):
        for copy in copies:
            copy.wait()
        from_w = jnp.where(lane == 0, unpack(lon_r[number, 0]), pltpu.roll(to_e, 1, 2))
        from_e = jnp.where(
            lane == wide - 1, unpack(lon_r[number, 1]), pltpu.roll(to_w, wide - 1, 2)
        )
        beyond = lat_r[number].astype(jnp.float32)
        hal[pl.ds(0, feats, stride=4), :] = beyond
        hal[pl.ds(3, feats, stride=4), :] = beyond
        edge = hal[...].reshape(cube)
        from_s = jnp.where(row == 0, jnp.where(south, 0.0, edge), pltpu.roll(to_n, 1, 1))
        from_n = jnp.where(row == 3, jnp.where(south, edge, 0.0), pltpu.roll(to_s, 7, 1))
        return [v.reshape(four) for v in (from_w, from_e, from_s, from_n)]

    def exchange(kind):
        copies = []
        for d in range(1, members):
            copies.append(
                pltpu.make_async_remote_copy(
                    snd.at[kind, partners[d]], rcv.at[kind, me],
                    a2a_ss.at[kind, d], a2a_rs.at[kind, d],
                    device_id=partner_ids[d], device_id_type=MESH,
                )
            )
            copies[-1].start()
        rcv[kind, me] = snd[kind, me]
        return copies

    def gathered(kind, side):
        return jnp.concatenate([rcv[kind, q, side] for q in range(members)], axis=1)

    def returned(kind, copies):
        for copy in copies:
            copy.wait()
        return jnp.concatenate(
            [rcv[kind, e % members, e // members] for e in range(experts)], axis=1
        )

    def keep(kind, side, slots):
        for q in range(members):
            snd[kind, q, side] = slots[:, q * cap : (q + 1) * cap]

    def halves(refs, which):
        return [
            ref.at[pl.ds(pl.multiple_of(which * (ref.shape[0] // 2), 64), ref.shape[0] // 2), :]
            for ref in refs
        ]

    def send_all(sources, targets, ss, rs, number, where):
        copies = [
            pltpu.make_async_remote_copy(
                src, dst, ss.at[number, i], rs.at[number, i],
                device_id=where, device_id_type=MESH,
            )
            for i, (src, dst) in enumerate(zip(sources, targets))
        ]
        for copy in copies:
            copy.start()
        return copies

    def columns_of(ref):
        return jnp.concatenate(
            [ref[pl.ds(i, feats, stride=4), :] for i in range(4)], axis=1
        ).astype(jnp.bfloat16)

    def to_slots(kind, columns):
        slots = matmul(columns, pt[...], (1, 1)).astype(jnp.bfloat16)
        for e in range(experts):
            snd[kind, e % members, e // members] = slots[:, e * cap : (e + 1) * cap]

    def to_grid(slots):
        columns = matmul(slots, pt[...], (1, 0))
        for i in range(4):
            tmp[pl.ds(i, feats, stride=4), :] = columns[:, i * wide : (i + 1) * wide]
        return tmp[...].reshape(four)

    loads["x"].wait()
    state = x_ref[...].reshape(four)
    whole = state.reshape(cube)
    pl.semaphore_wait(barrier, members - 1 + 3)
    copies = send_edges(0, whole, whole, whole, whole)
    for name in ("wo", "wi", "wm"):
        loads[name].wait()
    weights, far_weights = (wi_ref, wm_ref, wo_ref), (wi_far, wm_far, wo_far)
    sent_far = send_all(
        halves(weights, cl), halves(far_weights, cl), w_ss, w_rs, 0, far_id
    )

    for name in ("own", "cot"):
        loads[name].wait()
    count = 4 * wide
    owners = jnp.concatenate([own_ref[i : i + 1, :] for i in range(4)], axis=1)
    hot = (owners == lax.broadcasted_iota(jnp.int32, (experts, count), 0)).astype(jnp.float32)
    before = (
        lax.broadcasted_iota(jnp.int32, (count, count), 0)
        < lax.broadcasted_iota(jnp.int32, (count, count), 1)
    ).astype(jnp.float32).astype(jnp.bfloat16)
    earlier = matmul(hot.astype(jnp.bfloat16), before, (1, 0))
    rank = jnp.sum(hot * earlier, axis=0, keepdims=True)
    slot = owners * cap + rank.astype(jnp.int32)
    pt[...] = (
        lax.broadcasted_iota(jnp.int32, (experts * cap, count), 0) == slot
    ).astype(jnp.float32).astype(jnp.bfloat16)

    cot = cot_ref[...].reshape(four)
    tmp[...] = (act * cot).reshape(rows, wide)
    to_slots(0, columns_of(tmp))
    sent = exchange(0)

    for number in range(STEPS):
        if number > 0:
            whole = state.reshape(cube)
            copies = send_edges(number, whole, whole, whole, whole)
        from_w, from_e, from_s, from_n = shifted(number, copies, whole, whole, whole, whole)
        change = c_e * from_e + c_w * from_w + c_n * from_n + c_s * from_s
        state = state + act * (change - c_0 * state)
    adv_ref[...] = state.reshape(rows, wide)
    to_slots(1, columns_of(adv_ref))
    sent_in = exchange(1)
    stores[0].start()
    for copy in sent_far:
        copy.wait()
    sent_near = send_all(
        halves(far_weights, cl), halves(far_weights, cl), w_ss, w_rs, 1, cl_id
    )
    for copy in sent + sent_near + sent_in:
        copy.wait()

    sides = (1 - half, half)
    sets = (far_weights, weights)
    pushed = [gathered(0, side) for side in sides]
    inputs = [gathered(1, side) for side in sides]
    t_0 = [jnp.tanh(matmul(w[0][...], v, (0, 0))) for w, v in zip(sets, inputs)]
    a_0 = [t.astype(jnp.bfloat16) for t in t_0]
    back_2 = [matmul(w[2][...], v, (1, 0)) for w, v in zip(sets, pushed)]
    t_1 = [jnp.tanh(matmul(w[1][...], a, (0, 0))) for w, a in zip(sets, a_0)]
    a_1 = [t.astype(jnp.bfloat16) for t in t_1]
    delta_1 = [(b * (1.0 - t * t)).astype(jnp.bfloat16) for b, t in zip(back_2, t_1)]
    back_1 = [matmul(w[1][...], d, (1, 0)) for w, d in zip(sets, delta_1)]
    delta_0 = [(b * (1.0 - t * t)).astype(jnp.bfloat16) for b, t in zip(back_1, t_0)]
    for side, w, d in zip(sides, sets, delta_0):
        keep(2, side, matmul(w[0][...], d, (1, 0)).astype(jnp.bfloat16))
    sent_back = exchange(2)
    own, far = (gi_own, gm_own, go_own), (gi_far, gm_far, go_far)
    one, two = (gi_one, gm_one, go_one), (gi_two, gm_two, go_two)
    out, got = (gi_out, gm_out, go_out), (gi_got, gm_got, go_got)
    sums = (gi_ref, gm_ref, go_ref)
    sent_sums = []
    for i, (partial, landing) in enumerate(((far, two), (own, one))):
        partial[0][...] = matmul(inputs[i], delta_0[i], (1, 1))
        partial[1][...] = matmul(a_0[i], delta_1[i], (1, 1))
        partial[2][...] = matmul(a_1[i], pushed[i], (1, 1))
        sent_sums.append(send_all(halves(partial, 1 - cl), landing, g_ss, g_rs, i, cl_id))
    for side, w, a in zip(sides, sets, a_1):
        keep(3, side, matmul(w[2][...], a, (0, 0)).astype(jnp.bfloat16))
    for copy in sent_sums[0]:
        copy.wait()
    for target, mine, other in zip(out, halves(far, cl), two):
        target[...] = (mine[...] + other[...]).astype(jnp.bfloat16)
    sent_out = send_all(out, got, g_ss, g_rs, 2, far_id)

    grad = cot + to_grid(returned(2, sent_back))
    for number in range(STEPS, 2 * STEPS):
        held = act * grad
        parts = [(c * held).reshape(cube) for c in (c_e, c_w, c_n, c_s)]
        copies = send_edges(number, *parts)
        if number == STEPS:
            sent_raw = exchange(3)
        base = grad - c_0 * held
        if number == 2 * STEPS - 1:
            tend = returned(3, sent_raw)
        from_w, from_e, from_s, from_n = shifted(number, copies, *parts)
        grad = base + from_w + from_e + from_s + from_n
    sg_ref[...] = grad.reshape(rows, wide)
    stores[2].start()
    tend_ref[...] = (act * to_grid(tend)).reshape(rows, wide).astype(jnp.bfloat16)
    stores[1].start()
    for copy in sent_sums[1] + sent_out:
        copy.wait()
    for target, mine, a, b in zip(halves(sums, cl), halves(own, cl), one, got):
        target[...] = mine[...] + a[...] + b[...].astype(jnp.float32)
    for copy in send_all(halves(sums, cl), halves(sums, cl), g_ss, g_rs, 3, cl_id):
        copy.wait()
    for copy in stores[3:]:
        copy.start()
    for copy in stores:
        copy.wait()


def store_kernel(*refs):
    sems = refs[-1]
    loads = [pltpu.make_async_copy(refs[i], refs[i + 12], sems.at[0, i]) for i in range(6)]
    stores = [pltpu.make_async_copy(refs[i + 12], refs[i + 6], sems.at[1, i]) for i in range(6)]
    for copy in loads:
        copy.start()
    for load, store in zip(loads, stores):
        load.wait()
        store.start()
    for copy in stores:
        copy.wait()


def on_device_fused(
    ocean_state, cotangent, diffusivity, east_peclet, north_peclet, sea_mask, depth_levels,
    owner_table, w_in, w_mid, w_out,
):
    n_lon, n_lat, n_cl = (lax.axis_size(axis) for axis in ("lon", "lat", "cl"))
    wide = ocean_state.shape[3]
    rows = ocean_state.size // wide
    columns = 4 * wide
    experts = n_lon * n_lat
    cap = 2 * columns // experts
    feats, hidden = w_in.shape[1:]
    f32, bf16 = jnp.float32, jnp.bfloat16
    sizes = [(rows, wide)] * 3 + [(feats, hidden), (hidden, hidden), (hidden, feats)]
    results = [
        jax.ShapeDtypeStruct(size, bf16 if i == 1 else f32) for i, size in enumerate(sizes)
    ]
    flat = lambda v: v.reshape(-1, wide)
    hbm = pl.BlockSpec(memory_space=pltpu.HBM)
    operands = (
        flat(ocean_state), flat(cotangent), flat(diffusivity), flat(east_peclet),
        flat(north_peclet), sea_mask, depth_levels, flat(owner_table), w_in[0], w_mid[0, 0],
        w_out[0],
    )
    out = pl.pallas_call(
        functools.partial(tile_kernel, n_lon, n_lat, n_cl, cap),
        out_shape=results,
        in_specs=[hbm] * 11,
        out_specs=[hbm] * 6,
        scratch_shapes=[pltpu.VMEM(v.shape, v.dtype) for v in (*operands, *results)]
        + [
            pltpu.SemaphoreType.DMA((11,)),
            pltpu.SemaphoreType.DMA((6,)),
            pltpu.VMEM((2, 8, wide), jnp.int32),
            pltpu.VMEM((rows, wide), f32),
            pltpu.VMEM((rows, wide), f32),
            pltpu.VMEM((2 * STEPS, feats, wide), bf16),
            pltpu.VMEM((2 * STEPS, feats, wide), bf16),
            pltpu.VMEM((2 * STEPS, 2, 8, wide), f32),
            pltpu.VMEM((2 * STEPS, 2, 8, wide), f32),
            pltpu.VMEM((experts * cap, columns), bf16),
            pltpu.VMEM((4, experts // 2, 2, feats, cap), bf16),
            pltpu.VMEM((4, experts // 2, 2, feats, cap), bf16),
        ]
        + [pltpu.VMEM(size, bf16) for size in sizes[3:]]
        + [pltpu.VMEM(size, f32) for size in sizes[3:]] * 2
        + [pltpu.VMEM((size[0] // 2, size[1]), f32) for size in sizes[3:]] * 2
        + [pltpu.VMEM((size[0] // 2, size[1]), bf16) for size in sizes[3:]] * 2
        + [pltpu.SemaphoreType.DMA((2 * STEPS,))] * 2
        + [pltpu.SemaphoreType.DMA((2 * STEPS, 2))] * 2
        + [pltpu.SemaphoreType.DMA((4, experts // 2))] * 2
        + [pltpu.SemaphoreType.DMA((2, 3))] * 2
        + [pltpu.SemaphoreType.DMA((4, 3))] * 2,
        compiler_params=pltpu.CompilerParams(
            collective_id=0, has_side_effects=True, vmem_limit_bytes=VMEM_BYTES
        ),
    )(*operands)
    out = pl.pallas_call(
        store_kernel,
        out_shape=results,
        in_specs=[hbm] * 6,
        out_specs=[hbm] * 6,
        scratch_shapes=[pltpu.VMEM(v.shape, v.dtype) for v in results]
        + [pltpu.SemaphoreType.DMA((2, 6))],
        compiler_params=pltpu.CompilerParams(vmem_limit_bytes=VMEM_BYTES),
    )(*out)
    advected, tendency, state_grad, grad_in, grad_mid, grad_out = out
    shape = ocean_state.shape
    return (
        advected.reshape(shape), tendency.reshape(shape), state_grad.reshape(shape),
        grad_in[None], grad_mid[None, None], grad_out[None],
    )


def solution(mesh):
    few = mesh.shape["lat"] == 2 and mesh.shape["cl"] == 2 and mesh.shape["lon"] == 4
    plan = on_device_fused if few else on_device
    return jax.shard_map(
        plan,
        mesh=mesh,
        in_specs=(
            P("groups", None, "lat", ("lon", "cl")),
            P("groups", None, "lat", ("lon", "cl")),
            P(None, "lat", ("lon", "cl")),
            P(None, "lat", ("lon", "cl")),
            P(None, "lat", ("lon", "cl")),
            P("lat", ("lon", "cl")),
            P("lat", ("lon", "cl")),
            P("lat", ("lon", "cl"), None, None),
            P(("lon", "lat"), None, None),
            P(("lon", "lat"), None, None, None),
            P(("lon", "lat"), None, None),
        ),
        out_specs=(
            P("groups", None, "lat", ("lon", "cl")),
            P("groups", None, "lat", ("lon", "cl")),
            P("groups", None, "lat", ("lon", "cl")),
            P(("groups", "lon", "lat"), None, None),
            P(("groups", "lon", "lat"), None, None, None),
            P(("groups", "lon", "lat"), None, None),
        ),
        check_vma=False,
    )
```

```python
import functools

import jax
import jax.numpy as jnp
from jax import lax
from jax.experimental import pallas as pl
from jax.experimental.pallas import tpu as pltpu
from jax.sharding import PartitionSpec as P

STEPS = 2


def padded_2(value, sides, width, wrap):
    for axis, dim in sides:
        size, length = (lax.axis_size(axis), value.shape[dim])
        up = [(i, (i + 1) % size) for i in range(size if wrap else size - 1)]
        down = [(j, i) for i, j in up]
        last = lax.slice_in_dim(value, length - width, length, axis=dim)
        leading = lax.slice_in_dim(value, 0, width, axis=dim)
        before = lax.ppermute(last, axis, up)
        after = lax.ppermute(leading, axis, down)
        value = jnp.concatenate([before, value, after], axis=dim)
    return value


def build_table(diffusivity, east_peclet, north_peclet, sea_mask, depth_levels):
    levels = lax.broadcasted_iota(jnp.int32, diffusivity.shape, 0)
    active = (levels < depth_levels[None]).astype(jnp.float32) * sea_mask[None].astype(jnp.float32)
    return jnp.stack(
        [
            diffusivity * (1.0 - east_peclet),
            diffusivity * (1.0 + east_peclet),
            diffusivity * (1.0 - north_peclet),
            diffusivity * (1.0 + north_peclet),
            4.0 * diffusivity,
            active,
        ]
    )


def with_rims(grid_values, width):
    padded = padded_2(grid_values, (("lat", 2),), width, False)
    return padded_2(padded, ((("lon", "cl"), 3),), width, True)


def advance(padded, coefficients):
    inner_coef = coefficients[:, :, 1:-1, 1:-1]
    interior = padded[:, :, 1:-1, 1:-1]
    change = inner_coef[0] * padded[:, :, 1:-1, 2:] + inner_coef[1] * padded[:, :, 1:-1, :-2]
    change = (
        change + inner_coef[2] * padded[:, :, 2:, 1:-1] + inner_coef[3] * padded[:, :, :-2, 1:-1]
    )
    return interior + inner_coef[5] * (change - inner_coef[4] * interior)


def retreat(padded, coefficients):
    pushed = coefficients[5] * padded
    summed = padded[:, :, 1:-1, 1:-1] - (coefficients[4] * pushed)[:, :, 1:-1, 1:-1]
    summed = (
        summed
        + (coefficients[0] * pushed)[:, :, 1:-1, :-2]
        + (coefficients[1] * pushed)[:, :, 1:-1, 2:]
    )
    summed = (
        summed
        + (coefficients[2] * pushed)[:, :, :-2, 1:-1]
        + (coefficients[3] * pushed)[:, :, 2:, 1:-1]
    )
    return summed


def sweep_steps(grid_values, coefficients, update):
    for number in range(STEPS):
        grid_values = update(with_rims(grid_values, 1), coefficients)
    return grid_values


def project(left, right):
    return jnp.dot(left, right, preferred_element_type=jnp.float32)


def project_back(left, right):
    return lax.dot_general(
        left, right, (((1,), (1,)), ((), ())), preferred_element_type=jnp.float32
    )


def contract_rows(left, right):
    return lax.dot_general(
        left, right, (((0,), (0,)), ((), ())), preferred_element_type=jnp.float32
    )


def closure_pass(inputs, pushed, w_in, w_mid, w_out):
    slopes = []
    layers = [inputs]
    shaped = jnp.tanh(project(inputs, w_in))
    slopes.append(1.0 - shaped * shaped)
    acting = shaped.astype(jnp.bfloat16)
    layers.append(acting)
    layer_index = 0
    shaped = jnp.tanh(project(acting, w_mid[layer_index]))
    slopes.append(1.0 - shaped * shaped)
    acting = shaped.astype(jnp.bfloat16)
    layers.append(acting)
    raw_tend = project(acting, w_out).astype(jnp.bfloat16)
    grad_out = contract_rows(acting, pushed)
    backward = project_back(pushed, w_out)
    mid_grads = []
    for layer_index in reversed(range(w_mid.shape[0])):
        deltas = (backward * slopes[layer_index + 1]).astype(jnp.bfloat16)
        mid_grads.append(contract_rows(layers[layer_index + 1], deltas))
        backward = project_back(deltas, w_mid[layer_index])
    deltas = (backward * slopes[0]).astype(jnp.bfloat16)
    grad_in = contract_rows(inputs, deltas)
    back_in = project_back(deltas, w_in).astype(jnp.bfloat16)
    return (raw_tend, back_in, grad_in, jnp.stack(mid_grads[::-1]), grad_out)


def on_device(
    ocean_state,
    cotangent,
    diffusivity,
    east_peclet,
    north_peclet,
    sea_mask,
    depth_levels,
    owner_table,
    w_in,
    w_mid,
    w_out,
):
    coefficients = build_table(diffusivity, east_peclet, north_peclet, sea_mask, depth_levels)
    active = coefficients[5]
    rim_width = 1
    coef_rims = with_rims(coefficients, rim_width)
    advected = sweep_steps(ocean_state, coef_rims, advance)
    features = ocean_state.shape[0] * ocean_state.shape[1]
    columns = ocean_state.shape[2] * ocean_state.shape[3]
    experts = lax.axis_size(("lon", "lat"))
    capacity = 2 * columns // experts
    owners = owner_table.reshape(columns)
    one_hot = (owners[:, None] == lax.broadcasted_iota(jnp.int32, (columns, experts), 1)).astype(
        jnp.int32
    )
    rank_in = jnp.sum(jnp.cumsum(one_hot, axis=0) * one_hot, axis=1) - 1
    slot_index = owners * capacity + rank_in
    col_inputs = advected.reshape(features, columns).T.astype(jnp.bfloat16)
    col_pushed = (active[None] * cotangent).reshape(features, columns).T.astype(jnp.bfloat16)
    empty = jnp.zeros((experts * capacity, features), jnp.bfloat16)
    send_inputs = empty.at[slot_index].set(col_inputs)
    send_pushed = empty.at[slot_index].set(col_pushed)
    got_inputs, got_pushed = (
        lax.all_to_all(send_inputs, ("lon", "lat"), split_axis=0, concat_axis=0, tiled=True),
        lax.all_to_all(send_pushed, ("lon", "lat"), split_axis=0, concat_axis=0, tiled=True),
    )
    raw_tend, back_in, grad_in, grad_mid, grad_out = closure_pass(
        got_inputs, got_pushed, w_in[0], w_mid[0], w_out[0]
    )
    grad_in, grad_mid, grad_out = lax.psum((grad_in, grad_mid, grad_out), "cl")
    ret_tend, ret_back = (
        lax.all_to_all(raw_tend, ("lon", "lat"), split_axis=0, concat_axis=0, tiled=True),
        lax.all_to_all(back_in, ("lon", "lat"), split_axis=0, concat_axis=0, tiled=True),
    )
    tend_grid = ret_tend[slot_index].T.reshape(ocean_state.shape)
    back_grid = ret_back[slot_index].T.reshape(ocean_state.shape)
    tendency = (active[None] * tend_grid.astype(jnp.float32)).astype(jnp.bfloat16)
    adjoint_start = cotangent + back_grid.astype(jnp.float32)
    state_grad = sweep_steps(adjoint_start, coef_rims, retreat)
    return (advected, tendency, state_grad, grad_in[None], grad_mid[None], grad_out[None])


MESH = pl.DeviceIdType.MESH
VMEM_BYTES = 61 * 1024 * 1024


def matmul(left, right, contract):
    return lax.dot_general(
        left, right, (((contract[0],), (contract[1],)), ((), ())),
        preferred_element_type=jnp.float32,
    )


def tile_kernel(
    n_lon, n_lat, n_cl, cap,
    x_hbm, cot_hbm, diff_hbm, ep_hbm, np_hbm, sea_hbm, dep_hbm, own_hbm, wi_hbm, wm_hbm, wo_hbm,
    adv_hbm, tend_hbm, sg_hbm, gi_hbm, gm_hbm, go_hbm,
    x_ref, cot_ref, diff_ref, ep_ref, np_ref, sea_ref, dep_ref, own_ref, wi_ref, wm_ref, wo_ref,
    adv_ref, tend_ref, sg_ref, gi_ref, gm_ref, go_ref, load_sem, store_sem, d8, tmp, hal, lat_s, lat_r, lon_s, lon_r, pt, snd, rcv,
    wi_far, wm_far, wo_far, gi_own, gm_own, go_own, gi_far, gm_far, go_far,
    gi_one, gm_one, go_one, gi_two, gm_two, go_two,
    gi_out, gm_out, go_out, gi_got, gm_got, go_got,
    lat_ss, lat_rs, lon_ss, lon_rs, a2a_ss, a2a_rs, w_ss, w_rs, g_ss, g_rs,
):
    experts = n_lon * n_lat
    lon, lat, cl = lax.axis_index("lon"), lax.axis_index("lat"), lax.axis_index("cl")
    ring = n_lon * n_cl
    place = lon * n_cl + cl
    east, west = (place + 1) % ring, (place + ring - 1) % ring
    east_id = {"lon": east // n_cl, "cl": east % n_cl}
    west_id = {"lon": west // n_cl, "cl": west % n_cl}
    lat_id = {"lat": 1 - lat}
    cl_id = {"cl": 1 - cl}
    deep = n_lon // 2
    members = deep * n_lat
    half = lon // deep
    me = (lon % deep) * n_lat + lat
    partners = [(me + d) % members for d in range(members)]
    partner_ids = [{"lon": half * deep + p // n_lat, "lat": p % n_lat} for p in partners]
    far_id = {"lon": (lon + deep) % n_lon}

    barrier = pltpu.get_barrier_semaphore()
    for other in partner_ids[1:] + [east_id, west_id, far_id]:
        pl.semaphore_signal(barrier, inc=1, device_id=other, device_id_type=MESH)

    loads = {}
    for i, (name, src, dst) in enumerate((
        ("own", own_hbm, own_ref), ("x", x_hbm, x_ref), ("diff", diff_hbm, diff_ref), ("ep", ep_hbm, ep_ref),
        ("np", np_hbm, np_ref), ("sea", sea_hbm, sea_ref), ("dep", dep_hbm, dep_ref),
        ("cot", cot_hbm, cot_ref), ("wo", wo_hbm, wo_ref),
        ("wi", wi_hbm, wi_ref), ("wm", wm_hbm, wm_ref),
    )):
        loads[name] = pltpu.make_async_copy(src, dst, load_sem.at[i])
        loads[name].start()

    results = (
        (adv_ref, adv_hbm), (tend_ref, tend_hbm), (sg_ref, sg_hbm),
        (gi_ref, gi_hbm), (gm_ref, gm_hbm), (go_ref, go_hbm),
    )
    stores = [
        pltpu.make_async_copy(a, b, store_sem.at[i]) for i, (a, b) in enumerate(results)
    ]

    rows, wide = x_ref.shape
    tiles = rows // 8
    fields = rows // diff_ref.shape[0]
    feats = rows // 4
    cube = (tiles, 8, wide)
    four = (fields, tiles // fields, 8, wide)
    lane = lax.broadcasted_iota(jnp.int32, cube, 2)
    tile = lax.broadcasted_iota(jnp.int32, cube, 0)
    row = lax.broadcasted_iota(jnp.int32, cube, 1) % 4
    on_tile = lane == tile
    south = jnp.full(cube, lat, jnp.int32) == 0

    for name in ("sea", "dep", "diff", "ep", "np"):
        loads[name].wait()
    d8[0, 0:4], d8[0, 4:8] = sea_ref[...], sea_ref[...]
    d8[1, 0:4], d8[1, 4:8] = dep_ref[...], dep_ref[...]
    flat = (tiles // fields, 8, wide)
    level = 2 * lax.broadcasted_iota(jnp.int32, flat, 0) + (
        lax.broadcasted_iota(jnp.int32, flat, 1) // 4
    )
    diff = diff_ref[...].reshape(flat)
    ep, np_ = ep_ref[...].reshape(flat), np_ref[...].reshape(flat)
    active = (level < d8[1][None]).astype(jnp.float32) * d8[0][None].astype(jnp.float32)
    c_e, c_w = (diff * (1.0 - ep))[None], (diff * (1.0 + ep))[None]
    c_n, c_s = (diff * (1.0 - np_))[None], (diff * (1.0 + np_))[None]
    c_0, act = (4.0 * diff)[None], active[None]
    flat_lane = lax.broadcasted_iota(jnp.int32, flat, 2)
    flat_row = lax.broadcasted_iota(jnp.int32, flat, 1) % 4
    flat_south = jnp.full(flat, lat, jnp.int32) == 0
    a_e, a_w, a_n, a_s = act * c_e, act * c_w, act * c_n, act * c_s
    a_c = act * c_0
    rim_e = jnp.where(flat_lane == wide - 1, a_e[0], 0.0)[None]
    rim_w = jnp.where(flat_lane == 0, a_w[0], 0.0)[None]
    rim_lat = jnp.where(
        flat_south,
        jnp.where(flat_row == 3, a_n[0], 0.0),
        jnp.where(flat_row == 0, a_s[0], 0.0),
    )[None]

    def pack(value, side):
        return jnp.sum(jnp.where(on_tile, value[:, :, side : side + 1], 0.0), axis=0)

    def unpack(packed):
        return jnp.sum(jnp.where(on_tile, packed[None], 0.0), axis=2, keepdims=True)

    def fill_edges(number, to_e, to_w, to_n, to_s):
        tmp[...] = jnp.where(south, to_n, to_s).reshape(rows, wide)
        pick = jnp.full((feats, wide), lat, jnp.int32) == 0
        lat_s[number] = jnp.where(
            pick, tmp[pl.ds(3, feats, stride=4), :], tmp[pl.ds(0, feats, stride=4), :]
        ).astype(jnp.bfloat16)
        lon_s[number, 0] = pack(to_e, wide - 1)
        lon_s[number, 1] = pack(to_w, 0)

    def start_edges(number):
        copies = [
            pltpu.make_async_remote_copy(
                lat_s.at[number], lat_r.at[number], lat_ss.at[number], lat_rs.at[number],
                device_id=lat_id, device_id_type=MESH,
            ),
            pltpu.make_async_remote_copy(
                lon_s.at[number, 0], lon_r.at[number, 0],
                lon_ss.at[number, 0], lon_rs.at[number, 0],
                device_id=east_id, device_id_type=MESH,
            ),
            pltpu.make_async_remote_copy(
                lon_s.at[number, 1], lon_r.at[number, 1],
                lon_ss.at[number, 1], lon_rs.at[number, 1],
                device_id=west_id, device_id_type=MESH,
            ),
        ]
        for copy in copies:
            copy.start()
        return copies

    def inside(to_e, to_w, to_n, to_s):
        from_w = jnp.where(lane == 0, 0.0, pltpu.roll(to_e, 1, 2))
        from_e = jnp.where(lane == wide - 1, 0.0, pltpu.roll(to_w, wide - 1, 2))
        from_s = jnp.where(row == 0, 0.0, pltpu.roll(to_n, 1, 1))
        from_n = jnp.where(row == 3, 0.0, pltpu.roll(to_s, 7, 1))
        return [v.reshape(four) for v in (from_w, from_e, from_s, from_n)]

    def outside(number, copies):
        for copy in copies:
            copy.wait()
        beyond = lat_r[number].astype(jnp.float32)
        hal[pl.ds(0, feats, stride=4), :] = beyond
        hal[pl.ds(3, feats, stride=4), :] = beyond
        return (
            unpack(lon_r[number, 0]).reshape((*four[:3], 1)),
            unpack(lon_r[number, 1]).reshape((*four[:3], 1)),
            hal[...].reshape(four),
        )

    def exchange(kind):
        copies = []
        for d in range(1, members):
            copies.append(
                pltpu.make_async_remote_copy(
                    snd.at[kind, partners[d]], rcv.at[kind, me],
                    a2a_ss.at[kind, d], a2a_rs.at[kind, d],
                    device_id=partner_ids[d], device_id_type=MESH,
                )
            )
            copies[-1].start()
        rcv[kind, me] = snd[kind, me]
        return copies

    def gathered(kind, side):
        return jnp.concatenate([rcv[kind, q, side] for q in range(members)], axis=1)

    def returned(kind, copies):
        for copy in copies:
            copy.wait()
        return jnp.concatenate(
            [rcv[kind, e % members, e // members] for e in range(experts)], axis=1
        )

    def keep(kind, side, slots):
        for q in range(members):
            snd[kind, q, side] = slots[:, q * cap : (q + 1) * cap]

    def halves(refs, which):
        return [
            ref.at[pl.ds(pl.multiple_of(which * (ref.shape[0] // 2), 64), ref.shape[0] // 2), :]
            for ref in refs
        ]

    def send_all(sources, targets, ss, rs, number, where):
        copies = [
            pltpu.make_async_remote_copy(
                src, dst, ss.at[number, i], rs.at[number, i],
                device_id=where, device_id_type=MESH,
            )
            for i, (src, dst) in enumerate(zip(sources, targets))
        ]
        for copy in copies:
            copy.start()
        return copies

    def columns_of(ref):
        return jnp.concatenate(
            [ref[pl.ds(i, feats, stride=4), :] for i in range(4)], axis=1
        ).astype(jnp.bfloat16)

    def to_slots(kind, columns):
        slots = matmul(columns, pt[...], (1, 1)).astype(jnp.bfloat16)
        for e in range(experts):
            snd[kind, e % members, e // members] = slots[:, e * cap : (e + 1) * cap]

    def to_grid(slots):
        columns = matmul(slots, pt[...], (1, 0))
        for i in range(4):
            tmp[pl.ds(i, feats, stride=4), :] = columns[:, i * wide : (i + 1) * wide]
        return tmp[...].reshape(four)

    loads["own"].wait()
    count = 4 * wide
    owners = jnp.concatenate([own_ref[i : i + 1, :] for i in range(4)], axis=1)
    hot = (owners == lax.broadcasted_iota(jnp.int32, (experts, count), 0)).astype(jnp.float32)
    before = (
        lax.broadcasted_iota(jnp.int32, (count, count), 0)
        < lax.broadcasted_iota(jnp.int32, (count, count), 1)
    ).astype(jnp.float32).astype(jnp.bfloat16)
    earlier = matmul(hot.astype(jnp.bfloat16), before, (1, 0))
    rank = jnp.sum(hot * earlier, axis=0, keepdims=True)
    slot = owners * cap + rank.astype(jnp.int32)
    pt[...] = (
        lax.broadcasted_iota(jnp.int32, (experts * cap, count), 0) == slot
    ).astype(jnp.float32).astype(jnp.bfloat16)

    loads["x"].wait()
    state = x_ref[...].reshape(four)
    whole = state.reshape(cube)
    hal[...] = jnp.zeros_like(hal)
    fill_edges(0, whole, whole, whole, whole)
    pl.semaphore_wait(barrier, members - 1 + 3)
    copies = start_edges(0)
    for name in ("wo", "wi", "wm"):
        loads[name].wait()
    weights, far_weights = (wi_ref, wm_ref, wo_ref), (wi_far, wm_far, wo_far)
    sent_far = send_all(
        halves(weights, cl), halves(far_weights, cl), w_ss, w_rs, 0, far_id
    )

    loads["cot"].wait()
    cot = cot_ref[...].reshape(four)
    tmp[...] = (act * cot).reshape(rows, wide)
    to_slots(0, columns_of(tmp))
    sent = exchange(0)

    for number in range(STEPS):
        if number > 0:
            whole = state.reshape(cube)
            fill_edges(number, whole, whole, whole, whole)
            copies = start_edges(number)
        from_w, from_e, from_s, from_n = inside(whole, whole, whole, whole)
        state = state - a_c * state + (
            a_e * from_e + a_w * from_w + a_n * from_n + a_s * from_s
        )
        out_w, out_e, out_lat = outside(number, copies)
        state = state + (rim_w * out_w + rim_e * out_e + rim_lat * out_lat)
    adv_ref[...] = state.reshape(rows, wide)
    to_slots(1, columns_of(adv_ref))
    sent_in = exchange(1)
    stores[0].start()
    for copy in sent_far:
        copy.wait()
    sent_near = send_all(
        halves(far_weights, cl), halves(far_weights, cl), w_ss, w_rs, 1, cl_id
    )
    for copy in sent + sent_near + sent_in:
        copy.wait()

    sides = (1 - half, half)
    sets = (far_weights, weights)
    pushed = [gathered(0, side) for side in sides]
    inputs = [gathered(1, side) for side in sides]
    t_0 = [jnp.tanh(matmul(w[0][...], v, (0, 0))) for w, v in zip(sets, inputs)]
    a_0 = [t.astype(jnp.bfloat16) for t in t_0]
    back_2 = [matmul(w[2][...], v, (1, 0)) for w, v in zip(sets, pushed)]
    t_1 = [jnp.tanh(matmul(w[1][...], a, (0, 0))) for w, a in zip(sets, a_0)]
    a_1 = [t.astype(jnp.bfloat16) for t in t_1]
    delta_1 = [(b * (1.0 - t * t)).astype(jnp.bfloat16) for b, t in zip(back_2, t_1)]
    back_1 = [matmul(w[1][...], d, (1, 0)) for w, d in zip(sets, delta_1)]
    delta_0 = [(b * (1.0 - t * t)).astype(jnp.bfloat16) for b, t in zip(back_1, t_0)]
    for side, w, d in zip(sides, sets, delta_0):
        keep(2, side, matmul(w[0][...], d, (1, 0)).astype(jnp.bfloat16))
    sent_back = exchange(2)
    own, far = (gi_own, gm_own, go_own), (gi_far, gm_far, go_far)
    one, two = (gi_one, gm_one, go_one), (gi_two, gm_two, go_two)
    out, got = (gi_out, gm_out, go_out), (gi_got, gm_got, go_got)
    sums = (gi_ref, gm_ref, go_ref)
    sent_sums = []
    for i, (partial, landing) in enumerate(((far, two), (own, one))):
        partial[0][...] = matmul(inputs[i], delta_0[i], (1, 1))
        partial[1][...] = matmul(a_0[i], delta_1[i], (1, 1))
        partial[2][...] = matmul(a_1[i], pushed[i], (1, 1))
        sent_sums.append(send_all(halves(partial, 1 - cl), landing, g_ss, g_rs, i, cl_id))
    for side, w, a in zip(sides, sets, a_1):
        keep(3, side, matmul(w[2][...], a, (0, 0)).astype(jnp.bfloat16))
    for copy in sent_sums[0]:
        copy.wait()
    for target, mine, other in zip(out, halves(far, cl), two):
        target[...] = (mine[...] + other[...]).astype(jnp.bfloat16)
    sent_out = send_all(out, got, g_ss, g_rs, 2, far_id)

    four_lane = lane.reshape(four)
    four_rim = jnp.where(south, row, 3 - row).reshape(four) == 3
    grad = cot + to_grid(returned(2, sent_back))
    for number in range(STEPS, 2 * STEPS):
        held = act * grad
        parts = [(c * held).reshape(cube) for c in (c_e, c_w, c_n, c_s)]
        fill_edges(number, *parts)
        copies = start_edges(number)
        if number == STEPS:
            sent_raw = exchange(3)
        grad = grad - c_0 * held
        for part in inside(*parts):
            grad = grad + part
        out_w, out_e, out_lat = outside(number, copies)
        grad = grad + (
            jnp.where(four_lane == 0, out_w, 0.0)
            + jnp.where(four_lane == wide - 1, out_e, 0.0)
            + jnp.where(four_rim, out_lat, 0.0)
        )
    sg_ref[...] = grad.reshape(rows, wide)
    stores[2].start()
    for copy in sent_sums[1] + sent_out:
        copy.wait()
    for target, mine, a, b in zip(halves(sums, cl), halves(own, cl), one, got):
        target[...] = mine[...] + a[...] + b[...].astype(jnp.float32)
    sent_last = send_all(halves(sums, cl), halves(sums, cl), g_ss, g_rs, 3, cl_id)
    tend = returned(3, sent_raw)
    tend_ref[...] = (act * to_grid(tend)).reshape(rows, wide).astype(jnp.bfloat16)
    stores[1].start()
    for copy in sent_last:
        copy.wait()
    for copy in stores[3:]:
        copy.start()
    for copy in stores:
        copy.wait()


def store_kernel(*refs):
    sems = refs[-1]
    loads = [pltpu.make_async_copy(refs[i], refs[i + 12], sems.at[0, i]) for i in range(6)]
    stores = [pltpu.make_async_copy(refs[i + 12], refs[i + 6], sems.at[1, i]) for i in range(6)]
    for copy in loads:
        copy.start()
    for load, store in zip(loads, stores):
        load.wait()
        store.start()
    for copy in stores:
        copy.wait()


def on_device_fused(
    ocean_state, cotangent, diffusivity, east_peclet, north_peclet, sea_mask, depth_levels,
    owner_table, w_in, w_mid, w_out,
):
    n_lon, n_lat, n_cl = (lax.axis_size(axis) for axis in ("lon", "lat", "cl"))
    wide = ocean_state.shape[3]
    rows = ocean_state.size // wide
    columns = 4 * wide
    experts = n_lon * n_lat
    cap = 2 * columns // experts
    feats, hidden = w_in.shape[1:]
    f32, bf16 = jnp.float32, jnp.bfloat16
    sizes = [(rows, wide)] * 3 + [(feats, hidden), (hidden, hidden), (hidden, feats)]
    results = [
        jax.ShapeDtypeStruct(size, bf16 if i == 1 else f32) for i, size in enumerate(sizes)
    ]
    flat = lambda v: v.reshape(-1, wide)
    hbm = pl.BlockSpec(memory_space=pltpu.HBM)
    operands = (
        flat(ocean_state), flat(cotangent), flat(diffusivity), flat(east_peclet),
        flat(north_peclet), sea_mask, depth_levels, flat(owner_table), w_in[0], w_mid[0, 0],
        w_out[0],
    )
    out = pl.pallas_call(
        functools.partial(tile_kernel, n_lon, n_lat, n_cl, cap),
        out_shape=results,
        in_specs=[hbm] * 11,
        out_specs=[hbm] * 6,
        scratch_shapes=[pltpu.VMEM(v.shape, v.dtype) for v in (*operands, *results)]
        + [
            pltpu.SemaphoreType.DMA((11,)),
            pltpu.SemaphoreType.DMA((6,)),
            pltpu.VMEM((2, 8, wide), jnp.int32),
            pltpu.VMEM((rows, wide), f32),
            pltpu.VMEM((rows, wide), f32),
            pltpu.VMEM((2 * STEPS, feats, wide), bf16),
            pltpu.VMEM((2 * STEPS, feats, wide), bf16),
            pltpu.VMEM((2 * STEPS, 2, 8, wide), f32),
            pltpu.VMEM((2 * STEPS, 2, 8, wide), f32),
            pltpu.VMEM((experts * cap, columns), bf16),
            pltpu.VMEM((4, experts // 2, 2, feats, cap), bf16),
            pltpu.VMEM((4, experts // 2, 2, feats, cap), bf16),
        ]
        + [pltpu.VMEM(size, bf16) for size in sizes[3:]]
        + [pltpu.VMEM(size, f32) for size in sizes[3:]] * 2
        + [pltpu.VMEM((size[0] // 2, size[1]), f32) for size in sizes[3:]] * 2
        + [pltpu.VMEM((size[0] // 2, size[1]), bf16) for size in sizes[3:]] * 2
        + [pltpu.SemaphoreType.DMA((2 * STEPS,))] * 2
        + [pltpu.SemaphoreType.DMA((2 * STEPS, 2))] * 2
        + [pltpu.SemaphoreType.DMA((4, experts // 2))] * 2
        + [pltpu.SemaphoreType.DMA((2, 3))] * 2
        + [pltpu.SemaphoreType.DMA((4, 3))] * 2,
        compiler_params=pltpu.CompilerParams(
            collective_id=0, has_side_effects=True, vmem_limit_bytes=VMEM_BYTES
        ),
    )(*operands)
    out = pl.pallas_call(
        store_kernel,
        out_shape=results,
        in_specs=[hbm] * 6,
        out_specs=[hbm] * 6,
        scratch_shapes=[pltpu.VMEM(v.shape, v.dtype) for v in results]
        + [pltpu.SemaphoreType.DMA((2, 6))],
        compiler_params=pltpu.CompilerParams(vmem_limit_bytes=VMEM_BYTES),
    )(*out)
    advected, tendency, state_grad, grad_in, grad_mid, grad_out = out
    shape = ocean_state.shape
    return (
        advected.reshape(shape), tendency.reshape(shape), state_grad.reshape(shape),
        grad_in[None], grad_mid[None, None], grad_out[None],
    )


def solution(mesh):
    few = mesh.shape["lat"] == 2 and mesh.shape["cl"] == 2 and mesh.shape["lon"] == 4
    plan = on_device_fused if few else on_device
    return jax.shard_map(
        plan,
        mesh=mesh,
        in_specs=(
            P("groups", None, "lat", ("lon", "cl")),
            P("groups", None, "lat", ("lon", "cl")),
            P(None, "lat", ("lon", "cl")),
            P(None, "lat", ("lon", "cl")),
            P(None, "lat", ("lon", "cl")),
            P("lat", ("lon", "cl")),
            P("lat", ("lon", "cl")),
            P("lat", ("lon", "cl"), None, None),
            P(("lon", "lat"), None, None),
            P(("lon", "lat"), None, None, None),
            P(("lon", "lat"), None, None),
        ),
        out_specs=(
            P("groups", None, "lat", ("lon", "cl")),
            P("groups", None, "lat", ("lon", "cl")),
            P("groups", None, "lat", ("lon", "cl")),
            P(("groups", "lon", "lat"), None, None),
            P(("groups", "lon", "lat"), None, None, None),
            P(("groups", "lon", "lat"), None, None),
        ),
        check_vma=False,
    )
```

```python
import functools

import jax
import jax.numpy as jnp
from jax import lax
from jax.experimental import pallas as pl
from jax.experimental.pallas import tpu as pltpu
from jax.sharding import PartitionSpec as P

STEPS = 2


def padded_2(value, sides, width, wrap):
    for axis, dim in sides:
        size, length = (lax.axis_size(axis), value.shape[dim])
        up = [(i, (i + 1) % size) for i in range(size if wrap else size - 1)]
        down = [(j, i) for i, j in up]
        last = lax.slice_in_dim(value, length - width, length, axis=dim)
        leading = lax.slice_in_dim(value, 0, width, axis=dim)
        before = lax.ppermute(last, axis, up)
        after = lax.ppermute(leading, axis, down)
        value = jnp.concatenate([before, value, after], axis=dim)
    return value


def build_table(diffusivity, east_peclet, north_peclet, sea_mask, depth_levels):
    levels = lax.broadcasted_iota(jnp.int32, diffusivity.shape, 0)
    active = (levels < depth_levels[None]).astype(jnp.float32) * sea_mask[None].astype(jnp.float32)
    return jnp.stack(
        [
            diffusivity * (1.0 - east_peclet),
            diffusivity * (1.0 + east_peclet),
            diffusivity * (1.0 - north_peclet),
            diffusivity * (1.0 + north_peclet),
            4.0 * diffusivity,
            active,
        ]
    )


def with_rims(grid_values, width):
    padded = padded_2(grid_values, (("lat", 2),), width, False)
    return padded_2(padded, ((("lon", "cl"), 3),), width, True)


def advance(padded, coefficients):
    inner_coef = coefficients[:, :, 1:-1, 1:-1]
    interior = padded[:, :, 1:-1, 1:-1]
    change = inner_coef[0] * padded[:, :, 1:-1, 2:] + inner_coef[1] * padded[:, :, 1:-1, :-2]
    change = (
        change + inner_coef[2] * padded[:, :, 2:, 1:-1] + inner_coef[3] * padded[:, :, :-2, 1:-1]
    )
    return interior + inner_coef[5] * (change - inner_coef[4] * interior)


def retreat(padded, coefficients):
    pushed = coefficients[5] * padded
    summed = padded[:, :, 1:-1, 1:-1] - (coefficients[4] * pushed)[:, :, 1:-1, 1:-1]
    summed = (
        summed
        + (coefficients[0] * pushed)[:, :, 1:-1, :-2]
        + (coefficients[1] * pushed)[:, :, 1:-1, 2:]
    )
    summed = (
        summed
        + (coefficients[2] * pushed)[:, :, :-2, 1:-1]
        + (coefficients[3] * pushed)[:, :, 2:, 1:-1]
    )
    return summed


def sweep_steps(grid_values, coefficients, update):
    for number in range(STEPS):
        grid_values = update(with_rims(grid_values, 1), coefficients)
    return grid_values


def project(left, right):
    return jnp.dot(left, right, preferred_element_type=jnp.float32)


def project_back(left, right):
    return lax.dot_general(
        left, right, (((1,), (1,)), ((), ())), preferred_element_type=jnp.float32
    )


def contract_rows(left, right):
    return lax.dot_general(
        left, right, (((0,), (0,)), ((), ())), preferred_element_type=jnp.float32
    )


def closure_pass(inputs, pushed, w_in, w_mid, w_out):
    slopes = []
    layers = [inputs]
    shaped = jnp.tanh(project(inputs, w_in))
    slopes.append(1.0 - shaped * shaped)
    acting = shaped.astype(jnp.bfloat16)
    layers.append(acting)
    layer_index = 0
    shaped = jnp.tanh(project(acting, w_mid[layer_index]))
    slopes.append(1.0 - shaped * shaped)
    acting = shaped.astype(jnp.bfloat16)
    layers.append(acting)
    raw_tend = project(acting, w_out).astype(jnp.bfloat16)
    grad_out = contract_rows(acting, pushed)
    backward = project_back(pushed, w_out)
    mid_grads = []
    for layer_index in reversed(range(w_mid.shape[0])):
        deltas = (backward * slopes[layer_index + 1]).astype(jnp.bfloat16)
        mid_grads.append(contract_rows(layers[layer_index + 1], deltas))
        backward = project_back(deltas, w_mid[layer_index])
    deltas = (backward * slopes[0]).astype(jnp.bfloat16)
    grad_in = contract_rows(inputs, deltas)
    back_in = project_back(deltas, w_in).astype(jnp.bfloat16)
    return (raw_tend, back_in, grad_in, jnp.stack(mid_grads[::-1]), grad_out)


def on_device(
    ocean_state,
    cotangent,
    diffusivity,
    east_peclet,
    north_peclet,
    sea_mask,
    depth_levels,
    owner_table,
    w_in,
    w_mid,
    w_out,
):
    coefficients = build_table(diffusivity, east_peclet, north_peclet, sea_mask, depth_levels)
    active = coefficients[5]
    rim_width = 1
    coef_rims = with_rims(coefficients, rim_width)
    advected = sweep_steps(ocean_state, coef_rims, advance)
    features = ocean_state.shape[0] * ocean_state.shape[1]
    columns = ocean_state.shape[2] * ocean_state.shape[3]
    experts = lax.axis_size(("lon", "lat"))
    capacity = 2 * columns // experts
    owners = owner_table.reshape(columns)
    one_hot = (owners[:, None] == lax.broadcasted_iota(jnp.int32, (columns, experts), 1)).astype(
        jnp.int32
    )
    rank_in = jnp.sum(jnp.cumsum(one_hot, axis=0) * one_hot, axis=1) - 1
    slot_index = owners * capacity + rank_in
    col_inputs = advected.reshape(features, columns).T.astype(jnp.bfloat16)
    col_pushed = (active[None] * cotangent).reshape(features, columns).T.astype(jnp.bfloat16)
    empty = jnp.zeros((experts * capacity, features), jnp.bfloat16)
    send_inputs = empty.at[slot_index].set(col_inputs)
    send_pushed = empty.at[slot_index].set(col_pushed)
    got_inputs, got_pushed = (
        lax.all_to_all(send_inputs, ("lon", "lat"), split_axis=0, concat_axis=0, tiled=True),
        lax.all_to_all(send_pushed, ("lon", "lat"), split_axis=0, concat_axis=0, tiled=True),
    )
    raw_tend, back_in, grad_in, grad_mid, grad_out = closure_pass(
        got_inputs, got_pushed, w_in[0], w_mid[0], w_out[0]
    )
    grad_in, grad_mid, grad_out = lax.psum((grad_in, grad_mid, grad_out), "cl")
    ret_tend, ret_back = (
        lax.all_to_all(raw_tend, ("lon", "lat"), split_axis=0, concat_axis=0, tiled=True),
        lax.all_to_all(back_in, ("lon", "lat"), split_axis=0, concat_axis=0, tiled=True),
    )
    tend_grid = ret_tend[slot_index].T.reshape(ocean_state.shape)
    back_grid = ret_back[slot_index].T.reshape(ocean_state.shape)
    tendency = (active[None] * tend_grid.astype(jnp.float32)).astype(jnp.bfloat16)
    adjoint_start = cotangent + back_grid.astype(jnp.float32)
    state_grad = sweep_steps(adjoint_start, coef_rims, retreat)
    return (advected, tendency, state_grad, grad_in[None], grad_mid[None], grad_out[None])


MESH = pl.DeviceIdType.MESH
VMEM_BYTES = 61 * 1024 * 1024


def matmul(left, right, contract):
    return lax.dot_general(
        left, right, (((contract[0],), (contract[1],)), ((), ())),
        preferred_element_type=jnp.float32,
    )


def tile_kernel(
    n_lon, n_lat, n_cl, cap,
    x_hbm, cot_hbm, diff_hbm, ep_hbm, np_hbm, sea_hbm, dep_hbm, own_hbm, wi_hbm, wm_hbm, wo_hbm,
    adv_hbm, tend_hbm, sg_hbm, gi_hbm, gm_hbm, go_hbm,
    x_ref, cot_ref, diff_ref, ep_ref, np_ref, sea_ref, dep_ref, own_ref, wi_ref, wm_ref, wo_ref,
    adv_ref, tend_ref, sg_ref, gi_ref, gm_ref, go_ref, load_sem, store_sem, d8, tmp, hal, lat_s, lat_r, lon_s, lon_r, pt, snd, rcv,
    wi_far, wm_far, wo_far, gi_own, gm_own, go_own, gi_far, gm_far, go_far,
    gi_one, gm_one, go_one, gi_two, gm_two, go_two,
    gi_out, gm_out, go_out, gi_got, gm_got, go_got,
    lat_ss, lat_rs, lon_ss, lon_rs, a2a_ss, a2a_rs, w_ss, w_rs, g_ss, g_rs,
):
    experts = n_lon * n_lat
    lon, lat, cl = lax.axis_index("lon"), lax.axis_index("lat"), lax.axis_index("cl")
    ring = n_lon * n_cl
    place = lon * n_cl + cl
    east, west = (place + 1) % ring, (place + ring - 1) % ring
    east_id = {"lon": east // n_cl, "cl": east % n_cl}
    west_id = {"lon": west // n_cl, "cl": west % n_cl}
    lat_id = {"lat": 1 - lat}
    cl_id = {"cl": 1 - cl}
    deep = n_lon // 2
    members = deep * n_lat
    half = lon // deep
    me = (lon % deep) * n_lat + lat
    partners = [(me + d) % members for d in range(members)]
    partner_ids = [{"lon": half * deep + p // n_lat, "lat": p % n_lat} for p in partners]
    far_id = {"lon": (lon + deep) % n_lon}

    barrier = pltpu.get_barrier_semaphore()
    for other in partner_ids[1:] + [east_id, west_id, far_id]:
        pl.semaphore_signal(barrier, inc=1, device_id=other, device_id_type=MESH)

    loads = {}
    for i, (name, src, dst) in enumerate((
        ("own", own_hbm, own_ref), ("x", x_hbm, x_ref), ("diff", diff_hbm, diff_ref), ("ep", ep_hbm, ep_ref),
        ("np", np_hbm, np_ref), ("sea", sea_hbm, sea_ref), ("dep", dep_hbm, dep_ref),
        ("cot", cot_hbm, cot_ref), ("wo", wo_hbm, wo_ref),
        ("wi", wi_hbm, wi_ref), ("wm", wm_hbm, wm_ref),
    )):
        loads[name] = pltpu.make_async_copy(src, dst, load_sem.at[i])
        loads[name].start()

    results = (
        (adv_ref, adv_hbm), (tend_ref, tend_hbm), (sg_ref, sg_hbm),
        (gi_ref, gi_hbm), (gm_ref, gm_hbm), (go_ref, go_hbm),
    )
    stores = [
        pltpu.make_async_copy(a, b, store_sem.at[i]) for i, (a, b) in enumerate(results)
    ]

    rows, wide = x_ref.shape
    tiles = rows // 8
    fields = rows // diff_ref.shape[0]
    feats = rows // 4
    cube = (tiles, 8, wide)
    four = (fields, tiles // fields, 8, wide)
    lane = lax.broadcasted_iota(jnp.int32, cube, 2)
    tile = lax.broadcasted_iota(jnp.int32, cube, 0)
    row = lax.broadcasted_iota(jnp.int32, cube, 1) % 4
    on_tile = lane == tile
    south = jnp.full(cube, lat, jnp.int32) == 0

    for name in ("sea", "dep", "diff", "ep", "np"):
        loads[name].wait()
    d8[0, 0:4], d8[0, 4:8] = sea_ref[...], sea_ref[...]
    d8[1, 0:4], d8[1, 4:8] = dep_ref[...], dep_ref[...]
    flat = (tiles // fields, 8, wide)
    level = 2 * lax.broadcasted_iota(jnp.int32, flat, 0) + (
        lax.broadcasted_iota(jnp.int32, flat, 1) // 4
    )
    diff = diff_ref[...].reshape(flat)
    ep, np_ = ep_ref[...].reshape(flat), np_ref[...].reshape(flat)
    active = (level < d8[1][None]).astype(jnp.float32) * d8[0][None].astype(jnp.float32)
    c_e, c_w = (diff * (1.0 - ep))[None], (diff * (1.0 + ep))[None]
    c_n, c_s = (diff * (1.0 - np_))[None], (diff * (1.0 + np_))[None]
    c_0, act = (4.0 * diff)[None], active[None]
    flat_lane = lax.broadcasted_iota(jnp.int32, flat, 2)
    flat_row = lax.broadcasted_iota(jnp.int32, flat, 1) % 4
    flat_south = jnp.full(flat, lat, jnp.int32) == 0
    a_e, a_w, a_n, a_s = act * c_e, act * c_w, act * c_n, act * c_s
    a_c = act * c_0
    rim_e = jnp.where(flat_lane == wide - 1, a_e[0], 0.0)[None]
    rim_w = jnp.where(flat_lane == 0, a_w[0], 0.0)[None]
    rim_lat = jnp.where(
        flat_south,
        jnp.where(flat_row == 3, a_n[0], 0.0),
        jnp.where(flat_row == 0, a_s[0], 0.0),
    )[None]

    def pack(value, side):
        return jnp.sum(jnp.where(on_tile, value[:, :, side : side + 1], 0.0), axis=0)

    def unpack(packed):
        return jnp.sum(jnp.where(on_tile, packed[None], 0.0), axis=2, keepdims=True)

    def fill_edges(number, to_e, to_w, to_n, to_s):
        tmp[...] = jnp.where(south, to_n, to_s).reshape(rows, wide)
        pick = jnp.full((feats, wide), lat, jnp.int32) == 0
        lat_s[number] = jnp.where(
            pick, tmp[pl.ds(3, feats, stride=4), :], tmp[pl.ds(0, feats, stride=4), :]
        ).astype(jnp.bfloat16)
        lon_s[number, 0] = pack(to_e, wide - 1)
        lon_s[number, 1] = pack(to_w, 0)

    def start_edges(number):
        copies = [
            pltpu.make_async_remote_copy(
                lat_s.at[number], lat_r.at[number], lat_ss.at[number], lat_rs.at[number],
                device_id=lat_id, device_id_type=MESH,
            ),
            pltpu.make_async_remote_copy(
                lon_s.at[number, 0], lon_r.at[number, 0],
                lon_ss.at[number, 0], lon_rs.at[number, 0],
                device_id=east_id, device_id_type=MESH,
            ),
            pltpu.make_async_remote_copy(
                lon_s.at[number, 1], lon_r.at[number, 1],
                lon_ss.at[number, 1], lon_rs.at[number, 1],
                device_id=west_id, device_id_type=MESH,
            ),
        ]
        for copy in copies:
            copy.start()
        return copies

    def inside(to_e, to_w, to_n, to_s):
        from_w = jnp.where(lane == 0, 0.0, pltpu.roll(to_e, 1, 2))
        from_e = jnp.where(lane == wide - 1, 0.0, pltpu.roll(to_w, wide - 1, 2))
        from_s = jnp.where(row == 0, 0.0, pltpu.roll(to_n, 1, 1))
        from_n = jnp.where(row == 3, 0.0, pltpu.roll(to_s, 7, 1))
        return [v.reshape(four) for v in (from_w, from_e, from_s, from_n)]

    def outside(number, copies):
        for copy in copies:
            copy.wait()
        beyond = lat_r[number].astype(jnp.float32)
        hal[pl.ds(0, feats, stride=4), :] = beyond
        hal[pl.ds(3, feats, stride=4), :] = beyond
        return (
            unpack(lon_r[number, 0]).reshape((*four[:3], 1)),
            unpack(lon_r[number, 1]).reshape((*four[:3], 1)),
            hal[...].reshape(four),
        )

    def exchange(kind):
        copies = []
        for d in range(1, members):
            copies.append(
                pltpu.make_async_remote_copy(
                    snd.at[kind, partners[d]], rcv.at[kind, me],
                    a2a_ss.at[kind, d], a2a_rs.at[kind, d],
                    device_id=partner_ids[d], device_id_type=MESH,
                )
            )
            copies[-1].start()
        rcv[kind, me] = snd[kind, me]
        return copies

    def gathered(kind, side):
        return jnp.concatenate([rcv[kind, q, side] for q in range(members)], axis=1)

    def returned(kind, copies):
        for copy in copies:
            copy.wait()
        return jnp.concatenate(
            [rcv[kind, e % members, e // members] for e in range(experts)], axis=1
        )

    def keep(kind, side, slots):
        for q in range(members):
            snd[kind, q, side] = slots[:, q * cap : (q + 1) * cap]

    def halves(refs, which):
        return [
            ref.at[pl.ds(pl.multiple_of(which * (ref.shape[0] // 2), 64), ref.shape[0] // 2), :]
            for ref in refs
        ]

    def send_all(sources, targets, ss, rs, number, where):
        copies = [
            pltpu.make_async_remote_copy(
                src, dst, ss.at[number, i], rs.at[number, i],
                device_id=where, device_id_type=MESH,
            )
            for i, (src, dst) in enumerate(zip(sources, targets))
        ]
        for copy in copies:
            copy.start()
        return copies

    def columns_of(ref):
        return jnp.concatenate(
            [ref[pl.ds(i, feats, stride=4), :] for i in range(4)], axis=1
        ).astype(jnp.bfloat16)

    def to_slots(kind, columns):
        slots = matmul(columns, pt[...], (1, 1)).astype(jnp.bfloat16)
        for e in range(experts):
            snd[kind, e % members, e // members] = slots[:, e * cap : (e + 1) * cap]

    def to_grid(slots):
        columns = matmul(slots, pt[...], (1, 0))
        for i in range(4):
            tmp[pl.ds(i, feats, stride=4), :] = columns[:, i * wide : (i + 1) * wide]
        return tmp[...].reshape(four)

    loads["own"].wait()
    count = 4 * wide
    owners = jnp.concatenate([own_ref[i : i + 1, :] for i in range(4)], axis=1)
    hot = (owners == lax.broadcasted_iota(jnp.int32, (experts, count), 0)).astype(jnp.float32)
    before = (
        lax.broadcasted_iota(jnp.int32, (count, count), 0)
        < lax.broadcasted_iota(jnp.int32, (count, count), 1)
    ).astype(jnp.float32).astype(jnp.bfloat16)
    earlier = matmul(hot.astype(jnp.bfloat16), before, (1, 0))
    rank = jnp.sum(hot * earlier, axis=0, keepdims=True)
    slot = owners * cap + rank.astype(jnp.int32)
    pt[...] = (
        lax.broadcasted_iota(jnp.int32, (experts * cap, count), 0) == slot
    ).astype(jnp.float32).astype(jnp.bfloat16)

    loads["x"].wait()
    state = x_ref[...].reshape(four)
    whole = state.reshape(cube)
    hal[...] = jnp.zeros_like(hal)
    fill_edges(0, whole, whole, whole, whole)
    pl.semaphore_wait(barrier, members - 1 + 3)
    copies = start_edges(0)
    for name in ("wo", "wi", "wm"):
        loads[name].wait()
    weights, far_weights = (wi_ref, wm_ref, wo_ref), (wi_far, wm_far, wo_far)

    loads["cot"].wait()
    cot = cot_ref[...].reshape(four)
    tmp[...] = (act * cot).reshape(rows, wide)
    to_slots(0, columns_of(tmp))
    sent = exchange(0)

    for number in range(STEPS):
        if number > 0:
            whole = state.reshape(cube)
            fill_edges(number, whole, whole, whole, whole)
            copies = start_edges(number)
        if number == STEPS - 1:
            sent_far = send_all(
                halves(weights, cl), halves(far_weights, cl), w_ss, w_rs, 0, far_id
            )
        from_w, from_e, from_s, from_n = inside(whole, whole, whole, whole)
        state = state - a_c * state + (
            a_e * from_e + a_w * from_w + a_n * from_n + a_s * from_s
        )
        out_w, out_e, out_lat = outside(number, copies)
        state = state + (rim_w * out_w + rim_e * out_e + rim_lat * out_lat)
    adv_ref[...] = state.reshape(rows, wide)
    to_slots(1, columns_of(adv_ref))
    sent_in = exchange(1)
    stores[0].start()
    for copy in sent_far:
        copy.wait()
    sent_near = send_all(
        halves(far_weights, cl), halves(far_weights, cl), w_ss, w_rs, 1, cl_id
    )
    for copy in sent + sent_near + sent_in:
        copy.wait()

    sides = (1 - half, half)
    sets = (far_weights, weights)
    pushed = [gathered(0, side) for side in sides]
    inputs = [gathered(1, side) for side in sides]
    t_0 = [jnp.tanh(matmul(w[0][...], v, (0, 0))) for w, v in zip(sets, inputs)]
    a_0 = [t.astype(jnp.bfloat16) for t in t_0]
    back_2 = [matmul(w[2][...], v, (1, 0)) for w, v in zip(sets, pushed)]
    t_1 = [jnp.tanh(matmul(w[1][...], a, (0, 0))) for w, a in zip(sets, a_0)]
    a_1 = [t.astype(jnp.bfloat16) for t in t_1]
    delta_1 = [(b * (1.0 - t * t)).astype(jnp.bfloat16) for b, t in zip(back_2, t_1)]
    back_1 = [matmul(w[1][...], d, (1, 0)) for w, d in zip(sets, delta_1)]
    delta_0 = [(b * (1.0 - t * t)).astype(jnp.bfloat16) for b, t in zip(back_1, t_0)]
    for side, w, d in zip(sides, sets, delta_0):
        keep(2, side, matmul(w[0][...], d, (1, 0)).astype(jnp.bfloat16))
    sent_back = exchange(2)
    own, far = (gi_own, gm_own, go_own), (gi_far, gm_far, go_far)
    one, two = (gi_one, gm_one, go_one), (gi_two, gm_two, go_two)
    out, got = (gi_out, gm_out, go_out), (gi_got, gm_got, go_got)
    sums = (gi_ref, gm_ref, go_ref)
    sent_sums = []
    for i, (partial, landing) in enumerate(((far, two), (own, one))):
        partial[0][...] = matmul(inputs[i], delta_0[i], (1, 1))
        partial[1][...] = matmul(a_0[i], delta_1[i], (1, 1))
        partial[2][...] = matmul(a_1[i], pushed[i], (1, 1))
        sent_sums.append(send_all(halves(partial, 1 - cl), landing, g_ss, g_rs, i, cl_id))
    for side, w, a in zip(sides, sets, a_1):
        keep(3, side, matmul(w[2][...], a, (0, 0)).astype(jnp.bfloat16))
    for copy in sent_sums[0]:
        copy.wait()
    for target, mine, other in zip(out, halves(far, cl), two):
        target[...] = (mine[...] + other[...]).astype(jnp.bfloat16)
    sent_out = send_all(out, got, g_ss, g_rs, 2, far_id)

    four_lane = lane.reshape(four)
    four_rim = jnp.where(south, row, 3 - row).reshape(four) == 3
    grad = cot + to_grid(returned(2, sent_back))
    for number in range(STEPS, 2 * STEPS):
        held = act * grad
        parts = [(c * held).reshape(cube) for c in (c_e, c_w, c_n, c_s)]
        fill_edges(number, *parts)
        copies = start_edges(number)
        if number == STEPS:
            sent_raw = exchange(3)
        grad = grad - c_0 * held
        for part in inside(*parts):
            grad = grad + part
        out_w, out_e, out_lat = outside(number, copies)
        grad = grad + (
            jnp.where(four_lane == 0, out_w, 0.0)
            + jnp.where(four_lane == wide - 1, out_e, 0.0)
            + jnp.where(four_rim, out_lat, 0.0)
        )
    sg_ref[...] = grad.reshape(rows, wide)
    stores[2].start()
    for copy in sent_sums[1] + sent_out:
        copy.wait()
    for target, mine, a, b in zip(halves(sums, cl), halves(own, cl), one, got):
        target[...] = mine[...] + a[...] + b[...].astype(jnp.float32)
    sent_last = send_all(halves(sums, cl), halves(sums, cl), g_ss, g_rs, 3, cl_id)
    tend = returned(3, sent_raw)
    tend_ref[...] = (act * to_grid(tend)).reshape(rows, wide).astype(jnp.bfloat16)
    stores[1].start()
    for copy in sent_last:
        copy.wait()
    for copy in stores[3:]:
        copy.start()
    for copy in stores:
        copy.wait()


def store_kernel(*refs):
    sems = refs[-1]
    loads = [pltpu.make_async_copy(refs[i], refs[i + 12], sems.at[0, i]) for i in range(6)]
    stores = [pltpu.make_async_copy(refs[i + 12], refs[i + 6], sems.at[1, i]) for i in range(6)]
    for copy in loads:
        copy.start()
    for load, store in zip(loads, stores):
        load.wait()
        store.start()
    for copy in stores:
        copy.wait()


def on_device_fused(
    ocean_state, cotangent, diffusivity, east_peclet, north_peclet, sea_mask, depth_levels,
    owner_table, w_in, w_mid, w_out,
):
    n_lon, n_lat, n_cl = (lax.axis_size(axis) for axis in ("lon", "lat", "cl"))
    wide = ocean_state.shape[3]
    rows = ocean_state.size // wide
    columns = 4 * wide
    experts = n_lon * n_lat
    cap = 2 * columns // experts
    feats, hidden = w_in.shape[1:]
    f32, bf16 = jnp.float32, jnp.bfloat16
    sizes = [(rows, wide)] * 3 + [(feats, hidden), (hidden, hidden), (hidden, feats)]
    results = [
        jax.ShapeDtypeStruct(size, bf16 if i == 1 else f32) for i, size in enumerate(sizes)
    ]
    flat = lambda v: v.reshape(-1, wide)
    hbm = pl.BlockSpec(memory_space=pltpu.HBM)
    operands = (
        flat(ocean_state), flat(cotangent), flat(diffusivity), flat(east_peclet),
        flat(north_peclet), sea_mask, depth_levels, flat(owner_table), w_in[0], w_mid[0, 0],
        w_out[0],
    )
    out = pl.pallas_call(
        functools.partial(tile_kernel, n_lon, n_lat, n_cl, cap),
        out_shape=results,
        in_specs=[hbm] * 11,
        out_specs=[hbm] * 6,
        scratch_shapes=[pltpu.VMEM(v.shape, v.dtype) for v in (*operands, *results)]
        + [
            pltpu.SemaphoreType.DMA((11,)),
            pltpu.SemaphoreType.DMA((6,)),
            pltpu.VMEM((2, 8, wide), jnp.int32),
            pltpu.VMEM((rows, wide), f32),
            pltpu.VMEM((rows, wide), f32),
            pltpu.VMEM((2 * STEPS, feats, wide), bf16),
            pltpu.VMEM((2 * STEPS, feats, wide), bf16),
            pltpu.VMEM((2 * STEPS, 2, 8, wide), f32),
            pltpu.VMEM((2 * STEPS, 2, 8, wide), f32),
            pltpu.VMEM((experts * cap, columns), bf16),
            pltpu.VMEM((4, experts // 2, 2, feats, cap), bf16),
            pltpu.VMEM((4, experts // 2, 2, feats, cap), bf16),
        ]
        + [pltpu.VMEM(size, bf16) for size in sizes[3:]]
        + [pltpu.VMEM(size, f32) for size in sizes[3:]] * 2
        + [pltpu.VMEM((size[0] // 2, size[1]), f32) for size in sizes[3:]] * 2
        + [pltpu.VMEM((size[0] // 2, size[1]), bf16) for size in sizes[3:]] * 2
        + [pltpu.SemaphoreType.DMA((2 * STEPS,))] * 2
        + [pltpu.SemaphoreType.DMA((2 * STEPS, 2))] * 2
        + [pltpu.SemaphoreType.DMA((4, experts // 2))] * 2
        + [pltpu.SemaphoreType.DMA((2, 3))] * 2
        + [pltpu.SemaphoreType.DMA((4, 3))] * 2,
        compiler_params=pltpu.CompilerParams(
            collective_id=0, has_side_effects=True, vmem_limit_bytes=VMEM_BYTES
        ),
    )(*operands)
    out = pl.pallas_call(
        store_kernel,
        out_shape=results,
        in_specs=[hbm] * 6,
        out_specs=[hbm] * 6,
        scratch_shapes=[pltpu.VMEM(v.shape, v.dtype) for v in results]
        + [pltpu.SemaphoreType.DMA((2, 6))],
        compiler_params=pltpu.CompilerParams(vmem_limit_bytes=VMEM_BYTES),
    )(*out)
    advected, tendency, state_grad, grad_in, grad_mid, grad_out = out
    shape = ocean_state.shape
    return (
        advected.reshape(shape), tendency.reshape(shape), state_grad.reshape(shape),
        grad_in[None], grad_mid[None, None], grad_out[None],
    )


def solution(mesh):
    few = mesh.shape["lat"] == 2 and mesh.shape["cl"] == 2 and mesh.shape["lon"] == 4
    plan = on_device_fused if few else on_device
    return jax.shard_map(
        plan,
        mesh=mesh,
        in_specs=(
            P("groups", None, "lat", ("lon", "cl")),
            P("groups", None, "lat", ("lon", "cl")),
            P(None, "lat", ("lon", "cl")),
            P(None, "lat", ("lon", "cl")),
            P(None, "lat", ("lon", "cl")),
            P("lat", ("lon", "cl")),
            P("lat", ("lon", "cl")),
            P("lat", ("lon", "cl"), None, None),
            P(("lon", "lat"), None, None),
            P(("lon", "lat"), None, None, None),
            P(("lon", "lat"), None, None),
        ),
        out_specs=(
            P("groups", None, "lat", ("lon", "cl")),
            P("groups", None, "lat", ("lon", "cl")),
            P("groups", None, "lat", ("lon", "cl")),
            P(("groups", "lon", "lat"), None, None),
            P(("groups", "lon", "lat"), None, None, None),
            P(("groups", "lon", "lat"), None, None),
        ),
        check_vma=False,
    )
```
